256 devices in a mesh: tp: 16 (over y, x), pp: 16 (over z, core).
Axes of the slice: x: 4, y: 4, z: 8, core: 2. Of those that a mesh axis runs over, the one named last changes fastest.
Arguments:
- tokens: bfloat16 [16, 512, 8192], P('pp', None, 'tp'), may hold values from -28 to 28
- norm_gain: float32 [16, 8192], P('pp'), may hold values from 0.1 to 1.9
- w_query: bfloat16 [16, 8192, 4096], P('pp', None, 'tp'), may hold values from -2 to 2
- w_key: bfloat16 [16, 8192, 512], P('pp', None, 'tp'), may hold values from -1 to 1
- w_value: bfloat16 [16, 8192, 512], P('pp', None, 'tp'), may hold values from -0.0625 to 0.0625
- w_output: bfloat16 [16, 4096, 8192], P('pp', 'tp'), may hold values from -0.09375 to 0.09375
Outputs:
- handoff: float32 [16, 512, 8192], P('pp', None, 'tp')
The draws below stay inside these ranges and needn't reach their ends.
All inputs are finite; a program needn't handle non-finite values. Where the reference program divides by a largest or mean magnitude, that divisor is 1e-20 or more.
Results may differ from the reference program's by a relative error of at most 0.0065.
Values may be sent and summed in bfloat16 or wider, within the bound.
No kernel may reach another device: no remote copies, remote signals or barrier semaphores. Data moves between devices by JAX's collectives and lax.ppermute only.
A program may use at most 128 MiB of HBM per device.

```python
import math
import jax
import jax.numpy as jnp
from jax import lax

D = 8192
QH = 32
KVH = 4
HD = 128
BLOCK = 128
TOK = 512
SECTIONS = 16
GROUP = 8
N_TP = 16


def draw_tokens(key, part):
    key = jax.random.fold_in(key, 5)
    first = jax.random.fold_in(key, 0)
    values = jax.random.truncated_normal(first, -6.0, 6.0, (SECTIONS, TOK, D), jnp.float32)
    return jnp.clip(values, -28.0, 28.0).astype(jnp.bfloat16)


def draw_w_query(key, part):
    key = jax.random.fold_in(key, 11)
    first = jax.random.fold_in(key, 0)
    own = jax.random.truncated_normal(first, -6.0, 6.0, (SECTIONS, D, QH * HD), jnp.float32) * D ** (-0.5)
    values = own
    return jnp.clip(values, -2.0, 2.0).astype(jnp.bfloat16)


def draw_w_key(key, part):
    key = jax.random.fold_in(key, 17)
    values = jax.random.truncated_normal(key, -6.0, 6.0, (SECTIONS, D, KVH * HD), jnp.float32) * D ** (-0.5)
    return jnp.clip(values, -1.0, 1.0).astype(jnp.bfloat16)


def steps_of(key, extent, cuts, smallest, high):
    level = 1.0
    for position, blocks in cuts:
        heights = jax.random.uniform(jax.random.fold_in(jax.random.fold_in(key, 6), position), (blocks,), jnp.float32, smallest / len(cuts), high / len(cuts))
        level = level * jnp.repeat(jnp.exp(heights), extent[position] // blocks).reshape((-1,) + (1,) * (len(extent) - 1 - position))
    return level


def scatter_about(own_key, shape, scale, limit, shards=(), held_as=jnp.bfloat16):
    drawn = scale * jax.random.normal(own_key, shape, jnp.float32)
    if shards:
        drawn = drawn * steps_of(own_key, shape, shards, -0.22, 0.18)
    return jnp.clip(drawn, -limit, limit).astype(held_as)


def setup_inputs(seed: int = 0) -> dict:
    streams_of = jax.random.split(jax.random.key(seed), 7)
    tokens = draw_tokens(jax.random.fold_in(streams_of[6], 71), 0)
    norm_gain = jnp.clip(1.0 + 0.18 * jax.random.normal(streams_of[1], (SECTIONS, D), jnp.float32), 0.1, 1.9)
    w_query = draw_w_query(jax.random.fold_in(streams_of[6], 71), 0)
    w_key = draw_w_key(jax.random.fold_in(streams_of[6], 71), 0)
    w_value = scatter_about(streams_of[4], (SECTIONS, D, KVH * HD), D ** -0.5, 0.0625, ((0, 16), (2, 16)))
    w_output = scatter_about(streams_of[5], (SECTIONS, QH * HD, D), (QH * HD) ** -0.5, 0.09375, ((0, 16), (1, 16)))
    return dict(tokens=tokens, norm_gain=norm_gain, w_query=w_query, w_key=w_key, w_value=w_value, w_output=w_output)


def rotate(values, heads, head_size):
    rows = values.shape[0]
    half = head_size // 2
    freq = jnp.exp(jnp.arange(half, dtype=jnp.float32) * (-2.0 * math.log(500000.0) / head_size))
    angle = jnp.arange(rows, dtype=jnp.float32)[:, None] * freq[None, :]
    cosine = jnp.cos(angle)[:, None, :]
    sine = jnp.sin(angle)[:, None, :]
    shaped = values.reshape(rows, heads, head_size)
    first = shaped[..., :half]
    second = shaped[..., half:]
    return jnp.concatenate([first * cosine - second * sine, second * cosine + first * sine], axis=-1)

def quantize(values, block):
    rows, cols = values.shape
    blocks = values.reshape(rows, cols // block, block)
    scale = (lax.optimization_barrier(jnp.max(jnp.abs(blocks), axis=-1)) + 1e-06).astype(jnp.bfloat16)
    quant = (blocks / scale.astype(jnp.float32)[..., None]).astype(jnp.bfloat16)
    return (quant.reshape(rows, cols), scale)

def dequantize(quant, scale, block):
    rows, cols = quant.shape
    blocks = quant.astype(jnp.float32).reshape(rows, cols // block, block)
    return (blocks * scale.astype(jnp.float32)[..., None]).reshape(rows, cols)

def one_section(inputs):
    x_in, gain, w_q, w_k, w_v, w_o = inputs
    xf = x_in.astype(jnp.float32)
    normed = (xf * lax.rsqrt(lax.optimization_barrier(jnp.mean(xf * xf, axis=-1, keepdims=True)) + 1e-05) * gain).astype(jnp.bfloat16)
    queries = rotate(jnp.dot(normed, w_q, preferred_element_type=jnp.float32), QH, HD).astype(jnp.bfloat16)
    key_raw = jnp.dot(normed, w_k, preferred_element_type=jnp.float32).astype(jnp.bfloat16)
    value_raw = jnp.dot(normed, w_v, preferred_element_type=jnp.float32).astype(jnp.bfloat16)
    keys = rotate(key_raw.astype(jnp.float32), KVH, HD).astype(jnp.bfloat16)
    values = value_raw.reshape(TOK, KVH, HD)
    owner = jnp.arange(QH) // GROUP
    keys_h = keys[:, owner, :].astype(jnp.float32)
    values_h = values[:, owner, :].astype(jnp.float32)
    scores = jnp.einsum('thd,shd->hts', queries.astype(jnp.float32), keys_h) / math.sqrt(HD)
    causal = jnp.arange(TOK)[:, None] >= jnp.arange(TOK)[None, :]
    scores = jnp.where(causal[None], scores, jnp.float32(-1e+30))
    peak = lax.optimization_barrier(jnp.max(scores, axis=-1, keepdims=True))
    weights = jnp.exp(scores - peak)
    probs = (weights / lax.optimization_barrier(jnp.sum(weights, axis=-1, keepdims=True))).astype(jnp.bfloat16)
    context = jnp.einsum('hts,shd->thd', probs.astype(jnp.float32), values_h).astype(jnp.bfloat16)
    width = QH * HD // N_TP
    partial_value = jnp.einsum('tjc,jcd->jtd', context.reshape(TOK, N_TP, width).astype(jnp.float32), w_o.reshape(N_TP, width, D).astype(jnp.float32))
    quant, scale = quantize(partial_value.reshape(N_TP * TOK, D), BLOCK)
    attended = lax.optimization_barrier(jnp.sum(dequantize(quant, scale, BLOCK).reshape(N_TP, TOK, D), axis=0))
    merged = xf + attended
    out_quant, out_scale = quantize(merged, BLOCK)
    return dequantize(out_quant, out_scale, BLOCK)

def reference(tokens, norm_gain, w_query, w_key, w_value, w_output):
    results = lax.map(one_section, (tokens, norm_gain, w_query, w_key, w_value, w_output))
    return jnp.roll(results, 1, axis=0)
```

```python
import functools
import math

import jax
import jax.numpy as jnp
from jax import lax
from jax.experimental import pallas as pl
from jax.experimental.pallas import tpu as pltpu
from jax.sharding import Mesh
from jax.sharding import PartitionSpec as P

KVH = 4
HD = 128
SIDE = 4
EPS = 1e-05


def shift(block, axis, step):
    count = lax.axis_size(axis)
    return lax.ppermute(block, axis, [(i, (i + step) % count) for i in range(count)])


def dot(a, b, dims=((1,), (0,))):
    return lax.dot_general(a, b, (dims, ((), ())), preferred_element_type=jnp.float32)


def accumulate_kernel(pieces, first, last, width, table, *refs):
    refs = list(refs)
    take = lambda n: [refs.pop(0) for _ in range(n)]
    x_refs = take(pieces)
    gain, wq, wk, wv = take(4)
    prior = [] if first else take(3)
    tables = take(2) if last else []
    outs = take(2) if last else []
    sums = take(3)
    step = pl.program_id(0)

    @pl.when(step == 0)
    def _():
        for i, held in enumerate(sums):
            held[...] = jnp.zeros_like(held) if first else prior[i][...]

    q_sum, kv_sum, square_sum = sums
    x = jnp.concatenate([ref[...] for ref in x_refs], axis=0).astype(jnp.float32)
    squares = x * x
    total = squares[:, :128]
    for i in range(1, x.shape[1] // 128):
        total = total + squares[:, i * 128 : (i + 1) * 128]
    square_sum[...] += total
    scaled = (x * gain[...]).astype(jnp.bfloat16)
    q_sum[...] += dot(scaled, wq[...])
    kv_weights = jnp.concatenate([wk[...], wv[...]], axis=0)
    kv_sum[...] += dot(scaled, kv_weights, ((1,), (1,)))

    if last:
        cosine, sine = tables
        q_out, kv_out = outs

        @pl.when(step == pl.num_programs(0) - 1)
        def _():
            mean = jnp.sum(square_sum[...], axis=1, keepdims=True) / width
            row = lax.rsqrt(mean + EPS)
            kv_out[...] = (kv_sum[...] * row).astype(jnp.bfloat16)
            for h in range(q_sum.shape[1] // HD):
                one = q_sum[:, h * HD : (h + 1) * HD] * row
                turned = one * cosine[...] + pltpu.roll(one, HD // 2, 1) * sine[...]
                q_out[:, h * HD : (h + 1) * HD] = turned.astype(jnp.bfloat16)


def accumulate(pieces, table, gain, wq, wk, wv, prior=None, tables=None):
    rows = sum(p.shape[0] for p in pieces)
    depth = pieces[0].shape[1] // SIDE
    heads = wq.shape[1]
    narrow = 2 * wk.shape[0]
    first, last = prior is None, tables is not None
    fixed = lambda shape: pl.BlockSpec(shape, lambda k, t: (0, 0))
    in_specs = [pl.BlockSpec((p.shape[0], depth), lambda k, t: (0, k)) for p in pieces]
    in_specs += [
        pl.BlockSpec((1, depth), lambda k, t: (0, t[k])),
        pl.BlockSpec((depth, heads), lambda k, t: (t[k], 0)),
        pl.BlockSpec((wk.shape[0], depth), lambda k, t: (0, t[k])),
        pl.BlockSpec((wv.shape[0], depth), lambda k, t: (0, t[k])),
    ]
    args = list(pieces) + [gain, wq, wk, wv]
    sums = [(rows, heads), (rows, narrow), (rows, 128)]
    if not first:
        in_specs += [fixed(s) for s in sums]
        args += list(prior)
    if last:
        in_specs += [fixed(t.shape) for t in tables]
        args += list(tables)
        outs = [(s, jnp.bfloat16) for s in sums[:2]]
        scratch = [pltpu.VMEM(s, jnp.float32) for s in sums]
    else:
        outs = [(s, jnp.float32) for s in sums]
        scratch = []
    return pl.pallas_call(
        functools.partial(accumulate_kernel, len(pieces), first, last, gain.shape[1]),
        out_shape=[jax.ShapeDtypeStruct(s, d) for s, d in outs],
        grid_spec=pltpu.PrefetchScalarGridSpec(
            num_scalar_prefetch=1,
            grid=(SIDE,),
            in_specs=in_specs,
            out_specs=[fixed(s) for s, _ in outs],
            scratch_shapes=scratch,
        ),
        cost_estimate=pl.CostEstimate(
            flops=2 * rows * depth * SIDE * (heads + narrow),
            bytes_accessed=2 * SIDE * depth * (rows + heads + narrow) + 8 * rows * 448,
            transcendentals=0,
        ),
    )(table, *args)


def attend_kernel(start, place, q, own, right, two, left, cosine, sine, out):
    rows = q.shape[0]
    span = own.shape[0]
    part = own.shape[1] // 2
    line = lax.broadcasted_iota(jnp.int32, (2 * part, 2 * HD), 0)
    column = lax.broadcasted_iota(jnp.int32, (2 * part, 2 * HD), 1)
    home = jnp.where(line < part, line, line - part + HD)
    whole = jnp.zeros((span, 2 * HD), jnp.float32)
    for d, piece in enumerate((own, right, two, left)):
        at = lax.rem(place[0] + d, SIDE) * part
        whole += dot(piece[...], (column == home + at).astype(jnp.bfloat16))
    raw = whole[:, :HD]
    keys = (raw * cosine[...] + pltpu.roll(raw, HD // 2, 1) * sine[...]).astype(jnp.bfloat16)
    values = whole[:, HD:].astype(jnp.bfloat16)
    seen = (
        lax.broadcasted_iota(jnp.int32, (rows, span), 0) + start
        >= lax.broadcasted_iota(jnp.int32, (rows, span), 1)
    )
    for h in range(q.shape[1] // HD):
        scores = dot(q[:, h * HD : (h + 1) * HD], keys, ((1,), (1,))) * (1.0 / math.sqrt(HD))
        scores = jnp.where(seen, scores, jnp.float32(-1e30))
        weights = jnp.exp(scores - jnp.max(scores, axis=1, keepdims=True))
        probs = weights / jnp.sum(weights, axis=1, keepdims=True)
        out[:, h * HD : (h + 1) * HD] = dot(probs.astype(jnp.bfloat16), values).astype(
            jnp.bfloat16
        )


def attend(start, place, q, parts, cosine, sine):
    rows = q.shape[0]
    span = start + rows
    fixed = lambda shape: pl.BlockSpec(shape, lambda i, t: (0, 0))
    part = parts[0].shape[1]
    return pl.pallas_call(
        functools.partial(attend_kernel, start),
        out_shape=jax.ShapeDtypeStruct(q.shape, jnp.bfloat16),
        grid_spec=pltpu.PrefetchScalarGridSpec(
            num_scalar_prefetch=1,
            grid=(1,),
            in_specs=[fixed(q.shape)] + [fixed((span, part))] * 4 + [fixed((span, HD))] * 2,
            out_specs=fixed(q.shape),
        ),
        cost_estimate=pl.CostEstimate(
            flops=8 * rows * span * HD, bytes_accessed=4 * rows * 256, transcendentals=2 * rows * span
        ),
    )(place, q, *parts, cosine, sine)


def project_kernel(n_top, n_low, n_both, split, table, *refs):
    refs = list(refs)
    take = lambda n: [refs.pop(0) for _ in range(n)]
    context, weights = take(2)
    tops, lows, boths = take(n_top), take(n_low), take(n_both)
    half = context.shape[0] // 2
    value = dot(context[...], weights[...])
    top, low = value[:half], value[half:]
    for ref in tops:
        top = top + ref[...].astype(jnp.float32)
    for ref in lows:
        low = low + ref[...].astype(jnp.float32)
    for ref in boths:
        top = top + ref[:half].astype(jnp.float32)
        low = low + ref[half:].astype(jnp.float32)
    if split:
        refs[0][...] = top.astype(refs[0].dtype)
        refs[1][...] = low.astype(refs[1].dtype)
    else:
        refs[0][:half] = top.astype(refs[0].dtype)
        refs[0][half:] = low.astype(refs[0].dtype)


def project(context, weights, table, tops=(), lows=(), boths=(), split=False, kind=jnp.bfloat16):
    rows, depth = context.shape
    width = weights.shape[1] // SIDE**2
    half = rows // 2
    block = lambda r: pl.BlockSpec((r, width), lambda k, t: (0, k))
    shapes = [half, half] if split else [rows]
    result = pl.pallas_call(
        functools.partial(project_kernel, len(tops), len(lows), len(boths), split),
        out_shape=[jax.ShapeDtypeStruct((r, width * SIDE), kind) for r in shapes],
        grid_spec=pltpu.PrefetchScalarGridSpec(
            num_scalar_prefetch=1,
            grid=(SIDE,),
            in_specs=[
                pl.BlockSpec((rows, depth), lambda k, t: (0, 0)),
                pl.BlockSpec((depth, width), lambda k, t: (0, t[k])),
            ]
            + [block(half)] * (len(tops) + len(lows))
            + [block(rows)] * len(boths),
            out_specs=[block(r) for r in shapes],
        ),
        cost_estimate=pl.CostEstimate(
            flops=2 * rows * depth * width * SIDE,
            bytes_accessed=2 * SIDE * width * (depth + rows),
            transcendentals=0,
        ),
    )(table, context, weights, *tops, *lows, *boths)
    return result if split else result[0]


def ring_gather(block, axis):
    half = block.shape[0] // 2
    behind = shift(block, axis, 1)
    ahead = shift(block, axis, -1)
    far = (shift(behind[:half], axis, 1), shift(ahead[half:], axis, -1))
    return behind, ahead, far


def on_device(tokens, norm_gain, w_query, w_key, w_value, w_output):
    own = tokens[0]
    rows = own.shape[0]
    half = rows // 2
    y, x = lax.axis_index("ty"), lax.axis_index("tx")
    wq, wk, wv, wo = w_query[0], w_key[0].T, w_value[0].T, w_output[0]

    freq = jnp.exp(jnp.arange(HD // 2, dtype=jnp.float32) * (-2.0 * math.log(500000.0) / HD))
    angle = jnp.arange(rows, dtype=jnp.float32)[:, None] * freq[None, :]
    cosine = jnp.concatenate([jnp.cos(angle)] * 2, axis=1)
    sine = jnp.concatenate([-jnp.sin(angle), jnp.sin(angle)], axis=1)

    offsets = jnp.array((0, -1, 1, 2), jnp.int32)
    wrap = lambda v: (v + SIDE) % SIDE
    along = (
        lambda far: wrap(y + far) * SIDE + wrap(x + offsets),
        lambda far: wrap(y + offsets) * SIDE + wrap(x + far),
    )
    first_axis, second_axis = ("tx", "ty"), ("ty", "tx")

    blocks = [own[:half], own[half:]]
    near = [ring_gather(blocks[i], first_axis[i]) for i in range(2)]
    lines = [
        jnp.concatenate([blocks[i], near[i][0], near[i][1], jnp.concatenate(near[i][2])], axis=1)
        for i in range(2)
    ]
    distant = [ring_gather(lines[i], second_axis[i]) for i in range(2)]
    common = (norm_gain, wq, wk, wv)
    queries, narrow = [], []
    for i in range(2):
        sums = accumulate([lines[i]], along[i](0), *common)
        sums = accumulate([distant[i][0]], along[i](-1), *common, prior=sums)
        sums = accumulate([distant[i][1]], along[i](1), *common, prior=sums)
        cut = slice(i * half, (i + 1) * half)
        q, kv = accumulate(
            distant[i][2], along[i](2), *common, prior=sums, tables=(cosine[cut], sine[cut])
        )
        queries.append(q)
        narrow.append(kv)
    kv = jnp.concatenate(narrow)
    parts = (kv, shift(kv, "tx", -1), shift(kv, "tx", 2), shift(kv, "tx", 1))
    place = x.astype(jnp.int32)[None]
    merged = []
    contexts = [attend(i * half, place, queries[i], parts, cosine, sine) for i in range(2)]

    strips = []
    for i in range(2):
        axis = second_axis[i]
        run = functools.partial(project, contexts[i], wo)
        far_top, far_low = run(along[i](2), split=True)
        from_behind = shift(far_top, axis, 1)
        from_ahead = shift(far_low, axis, -1)
        onward = shift(run(along[i](1), tops=[from_behind]), axis, 1)
        back = shift(run(along[i](-1), lows=[from_ahead]), axis, -1)
        strips.append(run(along[i](0), boths=[onward, back], kind=jnp.float32))
    for i in range(2):
        axis = first_axis[i]
        width = strips[i].shape[1] // SIDE
        mine, behind, ahead, far = (strips[i][:, k * width : (k + 1) * width] for k in range(SIDE))
        cut = half // 2
        far = far.astype(jnp.bfloat16)
        from_behind = shift(far[:cut], axis, 1).astype(jnp.float32)
        from_ahead = shift(far[cut:], axis, -1).astype(jnp.float32)
        ahead = jnp.concatenate([ahead[:cut] + from_behind, ahead[cut:]]).astype(jnp.bfloat16)
        behind = jnp.concatenate([behind[:cut], behind[cut:] + from_ahead]).astype(jnp.bfloat16)
        onward, back = shift(ahead, axis, 1), shift(behind, axis, -1)
        merged.append(
            blocks[i].astype(jnp.float32)
            + (mine + onward.astype(jnp.float32) + back.astype(jnp.float32))
        )
    result = jnp.concatenate(merged).astype(jnp.bfloat16)
    return shift(result, "pp", 1).astype(jnp.float32)[None]


def solution(mesh):
    shape = mesh.devices.shape
    grid = Mesh(mesh.devices.reshape(SIDE, shape[0] // SIDE, shape[1]), ("ty", "tx", "pp"))
    tp = ("ty", "tx")
    return jax.shard_map(
        on_device,
        mesh=grid,
        in_specs=(
            P("pp", None, tp),
            P("pp", None),
            P("pp", None, tp),
            P("pp", None, tp),
            P("pp", None, tp),
            P("pp", tp, None),
        ),
        out_specs=P("pp", None, tp),
        check_vma=False,
    )
```

```python
import functools
import math

import jax
import jax.numpy as jnp
from jax import lax
from jax.experimental import pallas as pl
from jax.experimental.pallas import tpu as pltpu
from jax.sharding import Mesh
from jax.sharding import PartitionSpec as P

KVH = 4
HD = 128
SIDE = 4
EPS = 1e-05
OFFSETS = (0, -1, 1, 2)
VMEM_BYTES = 40 * 2**20


def shift(block, axis, step):
    count = lax.axis_size(axis)
    return lax.ppermute(block, axis, [(i, (i + step) % count) for i in range(count)])


def dot(a, b, dims=((1,), (0,))):
    return lax.dot_general(a, b, (dims, ((), ())), preferred_element_type=jnp.float32)


def call(kernel, table, args, specs, outs, flops, scratch=()):
    held = sum(math.prod(s.block_shape) for s in specs)
    return pl.pallas_call(
        kernel,
        out_shape=[jax.ShapeDtypeStruct(s, d) for s, d in outs],
        grid_spec=pltpu.PrefetchScalarGridSpec(
            num_scalar_prefetch=1,
            grid=(1,),
            in_specs=specs,
            out_specs=[whole(s) for s, _ in outs],
            scratch_shapes=scratch,
        ),
        compiler_params=pltpu.CompilerParams(vmem_limit_bytes=VMEM_BYTES),
        cost_estimate=pl.CostEstimate(flops=flops, bytes_accessed=4 * held, transcendentals=0),
    )(table, *args)


def whole(shape):
    return pl.BlockSpec(shape, lambda i, t: (0,) * len(shape))


def accumulate_kernel(half, pieces, first, last, width, table, *refs):
    refs = list(refs)
    take = lambda n: [refs.pop(0) for _ in range(n)]
    x_refs = [take(n) for n in pieces]
    weights = [take(4) for _ in range(2 * SIDE)]
    prior = [] if first else take(3)
    tables = take(2) if last else []
    outs = refs
    for i in range(2):
        rows = slice(i * half, (i + 1) * half)
        sums = [None if first else ref[rows] for ref in prior] or [None] * 3
        add = lambda k, value: value if sums[k] is None else sums[k] + value
        for k in range(SIDE):
            gain, wq, wk, wv = weights[i * SIDE + k]
            depth = wq.shape[0]
            cut = slice(k * depth, (k + 1) * depth)
            x = jnp.concatenate([ref[:, cut] for ref in x_refs[i]], axis=0).astype(jnp.float32)
            squares = x * x
            total = squares[:, :128]
            for j in range(1, depth // 128):
                total = total + squares[:, j * 128 : (j + 1) * 128]
            scaled = (x * gain[...]).astype(jnp.bfloat16)
            kv_weights = jnp.concatenate([wk[...], wv[...]], axis=0)
            sums = [
                add(0, dot(scaled, wq[...])),
                add(1, dot(scaled, kv_weights, ((1,), (1,)))),
                add(2, total),
            ]
        if not last:
            for ref, value in zip(outs, sums):
                ref[rows] = value
            continue
        cosine, sine = (t[rows] for t in tables)
        row = lax.rsqrt(jnp.sum(sums[2], axis=1, keepdims=True) / width + EPS)
        outs[1][rows] = (sums[1] * row).astype(jnp.bfloat16)
        for h in range(sums[0].shape[1] // HD):
            one = sums[0][:, h * HD : (h + 1) * HD] * row
            turned = one * cosine + pltpu.roll(one, HD // 2, 1) * sine
            outs[0][rows, h * HD : (h + 1) * HD] = turned.astype(jnp.bfloat16)


def accumulate(pieces, table, gain, wq, wk, wv, prior=None, tables=None):
    half = sum(p.shape[0] for p in pieces[0])
    depth = pieces[0][0].shape[1] // SIDE
    heads, narrow = wq.shape[1], 2 * wk.shape[0]
    args, specs = [], []
    for group in pieces:
        for p in group:
            args.append(p)
            specs.append(whole(p.shape))
    for k in range(2 * SIDE):
        args += [gain, wq, wk, wv]
        specs += [
            pl.BlockSpec((1, depth), lambda i, t, k=k: (0, t[k])),
            pl.BlockSpec((depth, heads), lambda i, t, k=k: (t[k], 0)),
            pl.BlockSpec((narrow // 2, depth), lambda i, t, k=k: (0, t[k])),
            pl.BlockSpec((narrow // 2, depth), lambda i, t, k=k: (0, t[k])),
        ]
    sums = [(2 * half, heads), (2 * half, narrow), (2 * half, 128)]
    for group in (prior, tables):
        if group is not None:
            args += list(group)
            specs += [whole(a.shape) for a in group]
    if tables is None:
        outs = [(s, jnp.float32) for s in sums]
    else:
        outs = [(s, jnp.bfloat16) for s in sums[:2]]
    kernel = functools.partial(
        accumulate_kernel,
        half,
        [len(g) for g in pieces],
        prior is None,
        tables is not None,
        gain.shape[1],
    )
    return call(kernel, table, args, specs, outs, 4 * half * depth * SIDE * (heads + narrow))


def attend_kernel(place, q, own, right, two, left, cosine, sine, out):
    rows = q.shape[0]
    half = rows // 2
    part = own.shape[1] // 2
    line = lax.broadcasted_iota(jnp.int32, (2 * part, 2 * HD), 0)
    column = lax.broadcasted_iota(jnp.int32, (2 * part, 2 * HD), 1)
    home = jnp.where(line < part, line, line - part + HD)
    both = jnp.zeros((rows, 2 * HD), jnp.float32)
    for d, piece in enumerate((own, right, two, left)):
        at = lax.rem(place[0] + d, SIDE) * part
        both += dot(piece[...], (column == home + at).astype(jnp.bfloat16))
    raw = both[:, :HD]
    keys = (raw * cosine[...] + pltpu.roll(raw, HD // 2, 1) * sine[...]).astype(jnp.bfloat16)
    values = both[:, HD:].astype(jnp.bfloat16)
    seen = lax.broadcasted_iota(jnp.int32, (half, half), 0) >= lax.broadcasted_iota(
        jnp.int32, (half, half), 1
    )
    for i in range(2):
        for h in range(q.shape[1] // HD):
            head = slice(h * HD, (h + 1) * HD)
            mine = q[i * half : (i + 1) * half, head]
            scores = []
            for j in range(i + 1):
                some = dot(mine, keys[j * half : (j + 1) * half], ((1,), (1,)))
                some = some * (1.0 / math.sqrt(HD))
                scores.append(jnp.where(seen, some, jnp.float32(-1e30)) if j == i else some)
            scores = jnp.concatenate(scores, axis=1)
            weights = jnp.exp(scores - jnp.max(scores, axis=1, keepdims=True))
            probs = weights * (1.0 / jnp.sum(weights, axis=1, keepdims=True))
            context = dot(probs.astype(jnp.bfloat16), values[: (i + 1) * half])
            out[i * half : (i + 1) * half, head] = context.astype(jnp.bfloat16)


def attend(place, q, parts, cosine, sine):
    args = [q, *parts, cosine, sine]
    specs = [whole(a.shape) for a in args]
    outs = [(q.shape, jnp.bfloat16)]
    return call(attend_kernel, place, args, specs, outs, 8 * q.shape[0] ** 2 * HD)[0]


def project_kernel(jobs, n_weights, table, context, *refs):
    refs = list(refs)
    weights = [refs.pop(0) for _ in range(n_weights)]
    adds = [[refs.pop(0) for _ in job["adds"]] for job in jobs]
    for job, extra in zip(jobs, adds):
        rows = job["rows"]
        sums = []
        for k in range(SIDE):
            weight = weights[job["weight"] * SIDE + k]
            width = weight.shape[1]
            value = dot(context[rows], weight[...])
            for ref, (_, cut) in zip(extra, job["adds"]):
                if ref.shape[1] == width:
                    more = ref[...] if k == 0 else None
                else:
                    more = ref[:, k * width : (k + 1) * width]
                if more is None:
                    continue
                more = more.astype(jnp.float32)
                if cut is None:
                    value = value + more
                elif cut == 0:
                    size = more.shape[0]
                    value = jnp.concatenate([value[:size] + more, value[size:]], axis=0)
                else:
                    value = jnp.concatenate([value[:cut], value[cut:] + more], axis=0)
            sums.append(value)
        if job["apart"]:
            for k in range(SIDE):
                ref = refs.pop(0)
                ref[...] = sums[k].astype(ref.dtype)
        else:
            ref = refs.pop(0)
            for k in range(SIDE):
                ref[:, k * width : (k + 1) * width] = sums[k].astype(ref.dtype)


def project(context, wo, table, jobs):
    depth = context.shape[1]
    width = wo.shape[1] // SIDE**2
    n_weights = table.shape[0]
    args, specs, outs = [context], [whole(context.shape)], []
    for k in range(n_weights):
        args.append(wo)
        specs.append(pl.BlockSpec((depth, width), lambda i, t, k=k: (0, t[k])))
    flops = 0
    for job in jobs:
        rows = job["rows"].stop - job["rows"].start
        flops += 2 * rows * depth * width * SIDE
        for a, _ in job["adds"]:
            args.append(a)
            specs.append(whole(a.shape))
        if job["apart"]:
            outs += [((rows, width), jnp.float32)] + [((rows, width), jnp.bfloat16)] * (SIDE - 1)
        else:
            outs.append(((rows, width * SIDE), jnp.bfloat16))
    return call(functools.partial(project_kernel, jobs, n_weights), table, args, specs, outs, flops)


def on_device(tokens, norm_gain, w_query, w_key, w_value, w_output):
    own = tokens[0]
    rows = own.shape[0]
    half, unit = rows // 2, rows // 4
    y, x = lax.axis_index("ty"), lax.axis_index("tx")
    wq, wk, wv, wo = w_query[0], w_key[0].T, w_value[0].T, w_output[0]

    freq = jnp.exp(jnp.arange(HD // 2, dtype=jnp.float32) * (-2.0 * math.log(500000.0) / HD))
    angle = jnp.arange(rows, dtype=jnp.float32)[:, None] * freq[None, :]
    cosine = jnp.concatenate([jnp.cos(angle)] * 2, axis=1)
    sine = jnp.concatenate([-jnp.sin(angle), jnp.sin(angle)], axis=1)

    wrap = lambda v: (v + SIDE) % SIDE
    offsets = jnp.array(OFFSETS, jnp.int32)
    owners = (
        lambda far: wrap(y + far) * SIDE + wrap(x + offsets),
        lambda far: wrap(y + offsets) * SIDE + wrap(x + far),
    )
    table = lambda *fars: jnp.concatenate([owners[i](far) for far in fars for i in range(2)])
    short, long = ("tx", "ty"), ("ty", "tx")

    tops, lows = [], []
    for i in range(2):
        block = own[i * half : (i + 1) * half]
        near = [block] + [shift(block, short[i], -d) for d in OFFSETS[1:]]
        tops.append(jnp.concatenate([b[:unit] for b in near], axis=1))
        lows.append(jnp.concatenate([b[unit:] for b in near], axis=1))
    common = (norm_gain, wq, wk, wv)
    behind = [[shift(tops[i], long[i], 1)] for i in range(2)]
    ahead = [[shift(lows[i], long[i], -1)] for i in range(2)]
    for i in range(2):
        behind[i].append(shift(lows[i], long[i], 1))
        ahead[i].insert(0, shift(tops[i], long[i], -1))
    far = [
        [shift(behind[i][0], long[i], 1), shift(ahead[i][1], long[i], -1)] for i in range(2)
    ]
    sums = accumulate([[tops[i], lows[i]] for i in range(2)], table(0), *common)
    sums = accumulate(behind, table(-1), *common, prior=sums)
    sums = accumulate(ahead, table(1), *common, prior=sums)
    queries, kv = accumulate(far, table(2), *common, prior=sums, tables=(cosine, sine))

    parts = [kv, shift(kv, "tx", -1), shift(kv, "tx", 2), shift(kv, "tx", 1)]
    context = attend(x.astype(jnp.int32)[None], queries, parts, cosine, sine)

    top = [slice(i * half, i * half + unit) for i in range(2)]
    low = [slice(i * half + unit, (i + 1) * half) for i in range(2)]
    full = [slice(i * half, (i + 1) * half) for i in range(2)]
    job = lambda rows, weight, adds=(), apart=False: dict(
        rows=rows, weight=weight, adds=list(adds), apart=apart
    )
    sent = project(
        context, wo, table(2), [job(r[i], i) for i in range(2) for r in (top, low)]
    )
    up = [shift(sent[2 * i], long[i], 1) for i in range(2)]
    down = [shift(sent[2 * i + 1], long[i], -1) for i in range(2)]
    sent = project(
        context,
        wo,
        table(1, -1),
        [j for i in range(2) for j in (job(low[i], i), job(top[i], 2 + i))],
    )
    up_low = [shift(sent[2 * i], long[i], 1) for i in range(2)]
    down_top = [shift(sent[2 * i + 1], long[i], -1) for i in range(2)]
    sent = project(
        context,
        wo,
        table(1, -1),
        [
            j
            for i in range(2)
            for j in (job(top[i], i, [(up[i], None)]), job(low[i], 2 + i, [(down[i], None)]))
        ],
    )
    up_top = [shift(sent[2 * i], long[i], 1) for i in range(2)]
    down_low = [shift(sent[2 * i + 1], long[i], -1) for i in range(2)]
    sent = project(
        context,
        wo,
        table(0),
        [
            job(
                full[i],
                i,
                [(up_top[i], 0), (down_top[i], 0), (up_low[i], unit), (down_low[i], unit)],
                True,
            )
            for i in range(2)
        ],
    )
    results = []
    for i in range(2):
        mine, *others = sent[SIDE * i : SIDE * (i + 1)]
        got = [shift(b, short[i], d) for b, d in zip(others, OFFSETS[1:])]
        merged = own[full[i]].astype(jnp.float32) + (
            mine + sum(g.astype(jnp.float32) for g in got)
        )
        results.append(shift(merged.astype(jnp.bfloat16), "pp", 1).astype(jnp.float32))
    return jnp.concatenate(results)[None]


def solution(mesh):
    shape = mesh.devices.shape
    grid = Mesh(mesh.devices.reshape(SIDE, shape[0] // SIDE, shape[1]), ("ty", "tx", "pp"))
    tp = ("ty", "tx")
    return jax.shard_map(
        on_device,
        mesh=grid,
        in_specs=(
            P("pp", None, tp),
            P("pp", None),
            P("pp", None, tp),
            P("pp", None, tp),
            P("pp", None, tp),
            P("pp", tp, None),
        ),
        out_specs=P("pp", None, tp),
        check_vma=False,
    )
```

```python
import functools
import math

import jax
import jax.numpy as jnp
import numpy as np
from jax import lax
from jax.experimental import pallas as pl
from jax.experimental.pallas import tpu as pltpu
from jax.sharding import Mesh
from jax.sharding import PartitionSpec as P

KVH = 4
HD = 128
SIDE = 4
EPS = 1e-05
COST = 16
VMEM_BYTES = 20 * 2**20

ROUNDS = (
    (
        ((-1, 0), (0, 0), "tx", 1),
        ((1, 0), (0, 0), "tx", -1),
        ((0, -1), (0, 0), "ty", 1),
        ((0, 1), (0, 0), "ty", -1),
    ),
    (
        ((-1, -1), (0, -1), "tx", 1),
        ((1, 1), (0, 1), "tx", -1),
        ((1, -1), (1, 0), "ty", 1),
        ((-1, 1), (-1, 0), "ty", -1),
    ),
    (
        ((2, 1), (1, 1), "tx", -1),
        ((2, -1), (-1, -1), "tx", 1),
        ((0, 2), (0, -1), "ty", 1),
        ((-1, 2), (-1, 1), "ty", -1),
    ),
    (
        ((2, 2), (2, 1), "ty", -1),
        ((1, 2), (1, -1), "ty", 1),
        ((2, 0), (1, 0), "tx", -1),
    ),
)
HOPS = {hop[0]: hop for hops in ROUNDS for hop in hops}
PLACES = [(0, 0)] + list(HOPS)
SUMS = (
    ((2, 2), (2, -1), (1, 2), (2, 0)),
    ((0, 2), (-1, 2)),
    ((2, 1),),
    ((-1, -1), (1, -1)),
    ((1, 1), (-1, 1)),
    ((1, 0), (0, -1)),
    ((-1, 0), (0, 1)),
)
AFTER = {(0, 2): (1, 2), (-1, 2): (2, 2), (1, -1): (0, 2)}


def shift(block, axis, step):
    count = lax.axis_size(axis)
    return lax.ppermute(block, axis, [(i, (i + step) % count) for i in range(count)])


def dot(a, b, dims=((1,), (0,))):
    return lax.dot_general(a, b, (dims, ((), ())), preferred_element_type=jnp.float32)


def call(kernel, table, args, specs, outs, flops, scratch=()):
    held = sum(math.prod(s.block_shape) for s in specs)
    return pl.pallas_call(
        kernel,
        out_shape=[jax.ShapeDtypeStruct(s, d) for s, d in outs],
        grid_spec=pltpu.PrefetchScalarGridSpec(
            num_scalar_prefetch=1,
            grid=(1,),
            in_specs=specs,
            out_specs=[whole(s) for s, _ in outs],
            scratch_shapes=scratch,
        ),
        compiler_params=pltpu.CompilerParams(vmem_limit_bytes=VMEM_BYTES),
        cost_estimate=pl.CostEstimate(flops=flops, bytes_accessed=4 * held, transcendentals=0),
    )(table, *args)


def whole(shape):
    return pl.BlockSpec(shape, lambda i, t: (0,) * len(shape))


def accumulate_kernel(count, first, last, width, table, *refs):
    refs = list(refs)
    take = lambda n: [refs.pop(0) for _ in range(n)]
    blocks = take(count)
    weights = [take(4) for _ in range(count)]
    prior = [] if first else take(3)
    tables = take(2) if last else []
    sums = [ref[...] for ref in prior] or [None] * 3
    for block, (gain, wq, wk, wv) in zip(blocks, weights):
        x = block[...].astype(jnp.float32)
        squares = x * x
        total = squares[:, :128]
        for j in range(1, x.shape[1] // 128):
            total = total + squares[:, j * 128 : (j + 1) * 128]
        scaled = (x * gain[...]).astype(jnp.bfloat16)
        kv_weights = jnp.concatenate([wk[...], wv[...]], axis=0)
        terms = (dot(scaled, wq[...]), dot(scaled, kv_weights, ((1,), (1,))), total)
        sums = [t if s is None else s + t for s, t in zip(sums, terms)]
    if not last:
        for ref, value in zip(refs, sums):
            ref[...] = value
        return
    cosine, sine = tables
    q, kv = refs
    row = lax.rsqrt(jnp.sum(sums[2], axis=1, keepdims=True) / width + EPS)
    kv[...] = (sums[1] * row).astype(jnp.bfloat16)
    for h in range(sums[0].shape[1] // HD):
        one = sums[0][:, h * HD : (h + 1) * HD] * row
        turned = one * cosine[...] + pltpu.roll(one, HD // 2, 1) * sine[...]
        q[:, h * HD : (h + 1) * HD] = turned.astype(jnp.bfloat16)


def accumulate(blocks, table, gain, wq, wk, wv, prior=None, tables=None):
    places, blocks = [PLACES.index(p) for p in blocks], list(blocks.values())
    count = len(blocks)
    rows, depth = blocks[0].shape
    heads, narrow = wq.shape[1], 2 * wk.shape[0]
    args = list(blocks)
    specs = [whole(b.shape) for b in blocks]
    for k in places:
        args += [gain, wq, wk, wv]
        specs += [
            pl.BlockSpec((1, depth), lambda i, t, k=k: (0, t[k])),
            pl.BlockSpec((depth, heads), lambda i, t, k=k: (t[k], 0)),
            pl.BlockSpec((narrow // 2, depth), lambda i, t, k=k: (0, t[k])),
            pl.BlockSpec((narrow // 2, depth), lambda i, t, k=k: (0, t[k])),
        ]
    for group in (prior, tables):
        if group is not None:
            args += list(group)
            specs += [whole(a.shape) for a in group]
    sums = [(rows, heads), (rows, narrow), (rows, 128)]
    if tables is None:
        outs = [(s, jnp.float32) for s in sums]
    else:
        outs = [(s, jnp.bfloat16) for s in sums[:2]]
    kernel = functools.partial(
        accumulate_kernel, count, prior is None, tables is not None, gain.shape[1]
    )
    return call(kernel, table, args, specs, outs, COST * rows * depth * count * (heads + narrow))


def attend_kernel(place, q, own, right, two, left, cosine, sine, out):
    rows = q.shape[0]
    half = rows // 2
    part = own.shape[1] // 2
    line = lax.broadcasted_iota(jnp.int32, (2 * part, 2 * HD), 0)
    column = lax.broadcasted_iota(jnp.int32, (2 * part, 2 * HD), 1)
    home = jnp.where(line < part, line, line - part + HD)
    both = jnp.zeros((rows, 2 * HD), jnp.float32)
    for d, piece in enumerate((own, right, two, left)):
        at = lax.rem(place[len(PLACES)] + d, SIDE) * part
        both += dot(piece[...], (column == home + at).astype(jnp.bfloat16))
    raw = both[:, :HD]
    keys = (raw * cosine[...] + pltpu.roll(raw, HD // 2, 1) * sine[...]).astype(jnp.bfloat16)
    values = both[:, HD:].astype(jnp.bfloat16)
    seen = lax.broadcasted_iota(jnp.int32, (half, half), 0) >= lax.broadcasted_iota(
        jnp.int32, (half, half), 1
    )
    for i in range(2):
        for h in range(q.shape[1] // HD):
            head = slice(h * HD, (h + 1) * HD)
            mine = q[i * half : (i + 1) * half, head]
            scores = []
            for j in range(i + 1):
                some = dot(mine, keys[j * half : (j + 1) * half], ((1,), (1,)))
                some = some * (1.0 / math.sqrt(HD))
                scores.append(jnp.where(seen, some, jnp.float32(-1e30)) if j == i else some)
            scores = jnp.concatenate(scores, axis=1)
            weights = jnp.exp(scores - jnp.max(scores, axis=1, keepdims=True))
            probs = weights * (1.0 / jnp.sum(weights, axis=1, keepdims=True))
            context = dot(probs.astype(jnp.bfloat16), values[: (i + 1) * half])
            out[i * half : (i + 1) * half, head] = context.astype(jnp.bfloat16)


def attend(place, q, parts, cosine, sine):
    args = [q, *parts, cosine, sine]
    specs = [whole(a.shape) for a in args]
    outs = [(q.shape, jnp.bfloat16)]
    return call(attend_kernel, place, args, specs, outs, 8 * q.shape[0] ** 2 * HD)[0]


def project_kernel(counts, base, table, context, *refs):
    refs = list(refs)
    take = lambda n: [refs.pop(0) for _ in range(n)]
    weights = take(len(counts))
    arrived = [take(n) for n in counts]
    residual = take(1) if base else []
    for weight, terms, out in zip(weights, arrived, refs):
        value = dot(context[...], weight[...])
        for term in terms + residual:
            value = value + term[...].astype(jnp.float32)
        out[...] = value.astype(out.dtype)


def project(context, wo, table, places, arrived, base=None):
    rows, depth = context.shape
    width = wo.shape[1] // SIDE**2
    args, specs = [context], [whole(context.shape)]
    for k in (PLACES.index(p) for p in places):
        args.append(wo)
        specs.append(pl.BlockSpec((depth, width), lambda i, t, k=k: (0, t[k])))
    more = [a for terms in arrived for a in terms] + ([] if base is None else [base])
    args += more
    specs += [whole(a.shape) for a in more]
    outs = [((rows, width), jnp.bfloat16)] * len(arrived)
    kernel = functools.partial(project_kernel, [len(t) for t in arrived], base is not None)
    return call(kernel, table, args, specs, outs, 2 * rows * depth * width * len(arrived))


def on_device(tokens, norm_gain, w_query, w_key, w_value, w_output):
    own = tokens[0]
    rows = own.shape[0]
    y, x = lax.axis_index("ty"), lax.axis_index("tx")
    wq, wk, wv, wo = w_query[0], w_key[0].T, w_value[0].T, w_output[0]

    freq = np.exp(np.arange(HD // 2) * (-2.0 * math.log(500000.0) / HD)).astype(np.float32)
    angle = np.arange(rows, dtype=np.float32)[:, None] * freq[None, :]
    cosine = np.concatenate([np.cos(angle)] * 2, axis=1)
    sine = np.concatenate([-np.sin(angle), np.sin(angle)], axis=1)

    dx = jnp.array([p[0] + SIDE for p in PLACES], jnp.int32)
    dy = jnp.array([p[1] + SIDE for p in PLACES], jnp.int32)
    owners = (y + dy) % SIDE * SIDE + (x + dx) % SIDE
    owners = jnp.concatenate([owners.astype(jnp.int32), x.astype(jnp.int32)[None]])

    common = (norm_gain, wq, wk, wv)
    held = {(0, 0): own}
    sums, group = None, [(0, 0)]
    for i, hops in enumerate(ROUNDS):
        for place, source, axis, step in hops:
            held[place] = shift(held[source], axis, step)
        group = group + [hop[0] for hop in hops]
        last = i == len(ROUNDS) - 1
        sums = accumulate(
            {p: held[p] for p in group},
            owners,
            *common,
            prior=sums,
            tables=(cosine, sine) if last else None,
        )
        group = []
    queries, kv = sums
    parts = [kv, shift(kv, "tx", -1), shift(kv, "tx", 2), shift(kv, "tx", 1)]
    context = attend(owners, queries, parts, cosine, sine)

    run = functools.partial(project, context, wo, owners)
    landed = {}
    terms = lambda place: [landed[p] for p in HOPS if HOPS[p][1] == place]
    for places in SUMS:
        for place, block in zip(places, run(places, [terms(p) for p in places])):
            _, _, axis, step = HOPS[place]
            if place in AFTER:
                earlier = AFTER[place]
                block, landed[earlier] = lax.optimization_barrier((block, landed[earlier]))
            landed[place] = shift(block, axis, -step)
    merged = run([(0, 0)], [terms((0, 0))], own)[0]
    return shift(merged, "pp", 1).astype(jnp.float32)[None]


def solution(mesh):
    shape = mesh.devices.shape
    grid = Mesh(mesh.devices.reshape(SIDE, shape[0] // SIDE, shape[1]), ("ty", "tx", "pp"))
    tp = ("ty", "tx")
    return jax.shard_map(
        on_device,
        mesh=grid,
        in_specs=(
            P("pp", None, tp),
            P("pp", None),
            P("pp", None, tp),
            P("pp", None, tp),
            P("pp", None, tp),
            P("pp", tp, None),
        ),
        out_specs=P("pp", None, tp),
        check_vma=False,
    )
```

```python
import functools
import math

import jax
import jax.numpy as jnp
import numpy as np
from jax import lax
from jax.experimental import pallas as pl
from jax.experimental.pallas import tpu as pltpu
from jax.sharding import Mesh
from jax.sharding import PartitionSpec as P

KVH = 4
HD = 128
SIDE = 4
SECTIONS = 16
EPS = 1e-05
COST = 16
VMEM_BYTES = 20 * 2**20

OFFSETS = (0, -1, 1, 2)


def route(axis_of_core, step):
    pairs = []
    for y in range(SIDE):
        for x in range(SIDE):
            for p in range(SECTIONS):
                along_x = axis_of_core[p % 2] == "tx"
                to_y = y if along_x else (y + step) % SIDE
                to_x = (x + step) % SIDE if along_x else x
                pairs.append(((y * SIDE + x) * SECTIONS + p, (to_y * SIDE + to_x) * SECTIONS + p))
    return pairs


def shift(block, axis_of_core, step):
    return lax.ppermute(block, ("ty", "tx", "pp"), route(axis_of_core, step))


SHORT = ("tx", "ty")
LONG = ("ty", "tx")
ROW = ("tx", "tx")


def dot(a, b, dims=((1,), (0,))):
    return lax.dot_general(a, b, (dims, ((), ())), preferred_element_type=jnp.float32)


def call(kernel, table, args, specs, outs, flops, scratch=()):
    held = sum(math.prod(s.block_shape) for s in specs)
    return pl.pallas_call(
        kernel,
        out_shape=[jax.ShapeDtypeStruct(s, d) for s, d in outs],
        grid_spec=pltpu.PrefetchScalarGridSpec(
            num_scalar_prefetch=1,
            grid=(1,),
            in_specs=specs,
            out_specs=[whole(s) for s, _ in outs],
            scratch_shapes=scratch,
        ),
        compiler_params=pltpu.CompilerParams(vmem_limit_bytes=VMEM_BYTES),
        cost_estimate=pl.CostEstimate(flops=flops, bytes_accessed=4 * held, transcendentals=0),
    )(table, *args)


def whole(shape):
    return pl.BlockSpec(shape, lambda i, t: (0,) * len(shape))


def accumulate_kernel(stacks, part, n_prior, n_extra, width, table, *refs):
    refs = list(refs)
    take = lambda n: [refs.pop(0) for _ in range(n)]
    blocks = []
    for ref, parts in zip(take(len(stacks)), stacks):
        rows = ref.shape[0] // parts
        blocks += [ref.at[pl.ds(n * rows, rows)] for n in range(parts)]
    weights = [take(2 if part == "q" else 4 if part == "all" else 3) for _ in blocks]
    prior, extra = take(n_prior), take(n_extra)
    sums = [ref[...] for ref in prior] or [None] * 3
    for block, (gain, *columns) in zip(blocks, weights):
        x = block[...].astype(jnp.float32)
        scaled = (x * gain[...]).astype(jnp.bfloat16)
        terms = []
        if part != "kv":
            terms.append(dot(scaled, columns[0][...]))
        if part != "q":
            kv_weights = jnp.concatenate([w[...] for w in columns[-2:]], axis=0)
            terms.append(dot(scaled, kv_weights, ((1,), (1,))))
            squares = x * x
            total = squares[:, :128]
            for j in range(1, x.shape[1] // 128):
                total = total + squares[:, j * 128 : (j + 1) * 128]
            terms.append(total)
        sums = [t if s is None else s + t for s, t in zip(sums, terms)]
    if part == "all":
        for ref, value in zip(refs, sums):
            ref[...] = value
    elif part == "kv":
        kv, factor = refs
        row = lax.rsqrt(jnp.sum(sums[1], axis=1, keepdims=True) / width + EPS)
        narrow = kv.shape[0]
        wide = jnp.concatenate([sums[0] * row, jnp.zeros((row.shape[0], HD - narrow), jnp.float32)], axis=1)
        kv[...] = wide.T[:narrow].astype(jnp.bfloat16)
        factor[...] = jnp.broadcast_to(row, factor.shape)
    else:
        factor, cosine, sine = extra
        (q,) = refs
        for h in range(q.shape[1] // HD):
            one = sums[0][:, h * HD : (h + 1) * HD] * factor[...]
            turned = one * cosine[...] + pltpu.roll(one, HD // 2, 1) * sine[...]
            q[:, h * HD : (h + 1) * HD] = turned.astype(jnp.bfloat16)


def accumulate(stacks, places, table, gain, wq, wk, wv, prior=(), extra=(), part="all"):
    count = len(places)
    depth = wq.shape[0] // SIDE**2
    rows = sum(s.shape[0] for s in stacks) // count
    parts = [s.shape[0] // rows for s in stacks]
    heads, narrow = wq.shape[1], 2 * wk.shape[0]
    args = list(stacks)
    specs = [whole(s.shape) for s in stacks]
    for k in places:
        args.append(gain)
        specs.append(pl.BlockSpec((1, depth), lambda i, t, k=k: (0, t[k])))
        if part != "kv":
            args.append(wq)
            specs.append(pl.BlockSpec((depth, heads), lambda i, t, k=k: (t[k], 0)))
        if part != "q":
            args += [wk, wv]
            specs += [pl.BlockSpec((narrow // 2, depth), lambda i, t, k=k: (0, t[k]))] * 2
    args += [*prior, *extra]
    specs += [whole(a.shape) for a in (*prior, *extra)]
    sums = [(rows, heads), (rows, narrow), (rows, HD)]
    outs = {
        "all": [(s, jnp.float32) for s in sums],
        "kv": [((narrow, rows), jnp.bfloat16), (sums[2], jnp.float32)],
        "q": [(sums[0], jnp.bfloat16)],
    }[part]
    kernel = functools.partial(
        accumulate_kernel, parts, part, len(prior), len(extra), gain.shape[1]
    )
    return call(kernel, table, args, specs, outs, COST * rows * depth * count * (heads + narrow))


def attend_kernel(place, q, own, right, two, left, cosine, sine, out, keys_raw, values):
    rows = q.shape[0]
    half = rows // 2
    part = own.shape[0] // 2
    for d, piece in enumerate((own, right, two, left)):
        at = pl.multiple_of(lax.rem(place[SIDE**2] + d, SIDE) * part, part)
        keys_raw[pl.ds(at, part), :] = piece[:part]
        values[pl.ds(at, part), :] = piece[part:]
    first = keys_raw[: HD // 2].astype(jnp.float32)
    second = keys_raw[HD // 2 :].astype(jnp.float32)
    keys = jnp.concatenate(
        [
            first * cosine[...] - second * sine[...],
            second * cosine[...] + first * sine[...],
        ],
        axis=0,
    ).astype(jnp.bfloat16)
    seen = lax.broadcasted_iota(jnp.int32, (half, half), 0) >= lax.broadcasted_iota(
        jnp.int32, (half, half), 1
    )
    for i in range(2):
        for h in range(q.shape[1] // HD):
            head = slice(h * HD, (h + 1) * HD)
            mine = q[i * half : (i + 1) * half, head]
            scores = []
            for j in range(i + 1):
                some = dot(mine, keys[:, j * half : (j + 1) * half]) * (1.0 / math.sqrt(HD))
                scores.append(jnp.where(seen, some, jnp.float32(-1e30)) if j == i else some)
            scores = jnp.concatenate(scores, axis=1)
            weights = jnp.exp(scores - jnp.max(scores, axis=1, keepdims=True))
            probs = weights * (1.0 / jnp.sum(weights, axis=1, keepdims=True))
            context = dot(probs.astype(jnp.bfloat16), values[:, : (i + 1) * half], ((1,), (1,)))
            out[i * half : (i + 1) * half, head] = context.astype(jnp.bfloat16)


def attend(place, q, parts, cosine, sine):
    args = [q, *parts, cosine, sine]
    specs = [whole(a.shape) for a in args]
    outs = [(q.shape, jnp.bfloat16)]
    scratch = [pltpu.VMEM((HD, q.shape[0]), jnp.bfloat16)] * 2
    return call(attend_kernel, place, args, specs, outs, 8 * q.shape[0] ** 2 * HD, scratch)[0]


def project_kernel(jobs, base, table, context, *refs):
    refs = list(refs)
    take = lambda n: [refs.pop(0) for _ in range(n)]
    weights = [take(len(job["places"])) for job in jobs]
    arrived = [take(len(job["adds"])) for job in jobs]
    residual = take(1) if base else []
    rows = context.shape[0]
    for job, group, terms in zip(jobs, weights, arrived):
        out = None if job["apart"] else refs.pop(0)
        for n, weight in enumerate(group):
            cut = pl.ds(n * rows, rows)
            value = dot(context[...], weight[...])
            for term in terms:
                value = value + term[cut].astype(jnp.float32)
            if not job["apart"]:
                out[cut] = value.astype(out.dtype)
                continue
            if residual:
                value = value + residual.pop()[...].astype(jnp.float32)
            alone = refs.pop(0)
            alone[...] = value.astype(alone.dtype)


def project(context, wo, table, jobs, base=None):
    rows, depth = context.shape
    width = wo.shape[1] // SIDE**2
    args, specs, outs = [context], [whole(context.shape)], []
    for job in jobs:
        for k in job["places"]:
            args.append(wo)
            specs.append(pl.BlockSpec((depth, width), lambda i, t, k=k: (0, t[k])))
        count = len(job["places"])
        if job["apart"]:
            outs += [((rows, width), jnp.bfloat16)] * count
        else:
            outs.append(((rows * count, width), jnp.bfloat16))
    if base is not None:
        outs[0] = (outs[0][0], jnp.float32)
    more = [a for job in jobs for a in job["adds"]] + ([] if base is None else [base])
    args += more
    specs += [whole(a.shape) for a in more]
    kernel = functools.partial(project_kernel, jobs, base is not None)
    count = sum(len(job["places"]) for job in jobs)
    return call(kernel, table, args, specs, outs, 2 * rows * depth * width * count)


def on_device(tokens, norm_gain, w_query, w_key, w_value, w_output):
    own = tokens[0]
    rows = own.shape[0]
    y, x = lax.axis_index("ty"), lax.axis_index("tx")
    wq, wk, wv, wo = w_query[0], w_key[0].T, w_value[0].T, w_output[0]

    freq = np.exp(np.arange(HD // 2) * (-2.0 * math.log(500000.0) / HD)).astype(np.float32)
    angle = np.arange(rows, dtype=np.float32)[:, None] * freq[None, :]
    cosine = np.concatenate([np.cos(angle)] * 2, axis=1)
    sine = np.concatenate([-np.sin(angle), np.sin(angle)], axis=1)

    far = jnp.array([f + SIDE for f in OFFSETS for _ in OFFSETS], jnp.int32)
    near = jnp.array([n + SIDE for _ in OFFSETS for n in OFFSETS], jnp.int32)
    x_first = lax.rem(lax.axis_index("pp"), 2) == 0
    owners = (y + jnp.where(x_first, far, near)) % SIDE * SIDE
    owners += (x + jnp.where(x_first, near, far)) % SIDE
    owners = jnp.concatenate([owners.astype(jnp.int32), x.astype(jnp.int32)[None]])
    spots = lambda far, *nears: [SIDE * OFFSETS.index(far) + OFFSETS.index(n) for n in nears]
    one, two = (0, -1), (1, 2)

    common = (owners, norm_gain, wq, wk, wv)
    behind, ahead, opposite = (shift(own, SHORT, -d) for d in OFFSETS[1:])
    first = jnp.concatenate([own, behind])
    first_up, first_down = shift(first, LONG, 1), shift(first, LONG, -1)
    second = jnp.concatenate([ahead, opposite])
    second_up, second_down = shift(second, LONG, 1), shift(second, LONG, -1)
    first_far, second_far = shift(first_up, LONG, 1), shift(second_down, LONG, -1)
    sums = accumulate([own, behind, ahead, opposite], spots(0, *one, *two), *common)
    sums = accumulate(
        [first_up, first_down], spots(-1, *one) + spots(1, *one), *common, prior=sums
    )
    sums = accumulate(
        [second_up, second_down], spots(-1, *two) + spots(1, *two), *common, prior=sums
    )
    stacks, places = [first_far, second_far], spots(2, *one, *two)
    kv, row = accumulate(stacks, places, *common, prior=sums[1:], part="kv")
    queries = accumulate(
        stacks, places, *common, prior=sums[:1], extra=(row, cosine, sine), part="q"
    )[0]
    parts = [kv, shift(kv, ROW, -1), shift(kv, ROW, 2), shift(kv, ROW, 1)]
    context = attend(owners, queries, parts, np.cos(angle).T.copy(), np.sin(angle).T.copy())

    job = lambda far, nears, adds=(), apart=False: dict(
        places=spots(far, *nears), adds=list(adds), apart=apart
    )
    sent = project(context, wo, owners, [job(2, one), job(2, two)])
    up, down = shift(sent[0], LONG, 1), shift(sent[1], LONG, -1)
    context, _ = lax.optimization_barrier((context, sent[0]))
    run = functools.partial(project, context, wo, owners)
    sent = run([job(1, two), job(-1, one)])
    two_up, one_down = shift(sent[0], LONG, 1), shift(sent[1], LONG, -1)
    one_up = shift(run([job(1, one, [up])])[0], LONG, 1)
    two_down = shift(run([job(-1, two, [down])])[0], LONG, -1)
    jobs = [job(0, one, [one_up, one_down], True), job(0, two, [two_up, two_down], True)]
    mine, *others = run(jobs, own)
    for d, block in zip(OFFSETS[1:], others):
        mine = mine + shift(block, SHORT, d).astype(jnp.float32)
    step = [(p, (p + 1) % SECTIONS) for p in range(SECTIONS)]
    return lax.ppermute(mine.astype(jnp.bfloat16), "pp", step).astype(jnp.float32)[None]


def solution(mesh):
    shape = mesh.devices.shape
    grid = Mesh(mesh.devices.reshape(SIDE, shape[0] // SIDE, shape[1]), ("ty", "tx", "pp"))
    tp = ("ty", "tx")
    return jax.shard_map(
        on_device,
        mesh=grid,
        in_specs=(
            P("pp", None, tp),
            P("pp", None),
            P("pp", None, tp),
            P("pp", None, tp),
            P("pp", None, tp),
            P("pp", tp, None),
        ),
        out_specs=P("pp", None, tp),
        check_vma=False,
    )
```

```python
import functools
import math

import jax
import jax.numpy as jnp
import numpy as np
from jax import lax
from jax.experimental import pallas as pl
from jax.experimental.pallas import tpu as pltpu
from jax.sharding import Mesh
from jax.sharding import PartitionSpec as P

KVH = 4
HD = 128
SIDE = 4
SECTIONS = 16
EPS = 1e-05
COST = 16
VMEM_BYTES = 20 * 2**20

OFFSETS = (0, -1, 1, 2)


def route(axis_of_core, step):
    pairs = []
    for y in range(SIDE):
        for x in range(SIDE):
            for p in range(SECTIONS):
                along_x = axis_of_core[p % 2] == "tx"
                to_y = y if along_x else (y + step) % SIDE
                to_x = (x + step) % SIDE if along_x else x
                pairs.append(((y * SIDE + x) * SECTIONS + p, (to_y * SIDE + to_x) * SECTIONS + p))
    return pairs


def shift(block, axis_of_core, step):
    return lax.ppermute(block, ("ty", "tx", "pp"), route(axis_of_core, step))


SHORT = ("tx", "ty")
LONG = ("ty", "tx")
ROW = ("tx", "tx")


def dot(a, b, dims=((1,), (0,))):
    return lax.dot_general(a, b, (dims, ((), ())), preferred_element_type=jnp.float32)


def call(kernel, table, args, specs, outs, flops, scratch=()):
    held = sum(math.prod(s.block_shape) for s in specs)
    return pl.pallas_call(
        kernel,
        out_shape=[jax.ShapeDtypeStruct(s, d) for s, d in outs],
        grid_spec=pltpu.PrefetchScalarGridSpec(
            num_scalar_prefetch=1,
            grid=(1,),
            in_specs=specs,
            out_specs=[whole(s) for s, _ in outs],
            scratch_shapes=scratch,
        ),
        compiler_params=pltpu.CompilerParams(vmem_limit_bytes=VMEM_BYTES),
        cost_estimate=pl.CostEstimate(flops=flops, bytes_accessed=4 * held, transcendentals=0),
    )(table, *args)


def whole(shape):
    return pl.BlockSpec(shape, lambda i, t: (0,) * len(shape))


def accumulate_kernel(stacks, part, n_prior, n_extra, width, table, *refs):
    refs = list(refs)
    take = lambda n: [refs.pop(0) for _ in range(n)]
    blocks = []
    for ref, parts in zip(take(len(stacks)), stacks):
        rows = ref.shape[0] // parts
        blocks += [ref.at[pl.ds(n * rows, rows)] for n in range(parts)]
    weights = [take(2 if part == "q" else 4 if part == "all" else 3) for _ in blocks]
    prior, extra = take(n_prior), take(n_extra)
    sums = [ref[...] for ref in prior] or [None] * 3
    for block, (gain, *columns) in zip(blocks, weights):
        x = block[...].astype(jnp.float32)
        scaled = (x * gain[...]).astype(jnp.bfloat16)
        terms = []
        if part != "kv":
            terms.append(dot(scaled, columns[0][...]))
        if part != "q":
            kv_weights = jnp.concatenate([w[...] for w in columns[-2:]], axis=0)
            terms.append(dot(scaled, kv_weights, ((1,), (1,))))
            squares = x * x
            total = squares[:, :128]
            for j in range(1, x.shape[1] // 128):
                total = total + squares[:, j * 128 : (j + 1) * 128]
            terms.append(total)
        sums = [t if s is None else s + t for s, t in zip(sums, terms)]
    if part == "all":
        for ref, value in zip(refs, sums):
            ref[...] = value
    elif part == "kv":
        kv, factor = refs
        row = lax.rsqrt(jnp.sum(sums[1], axis=1, keepdims=True) / width + EPS)
        narrow = kv.shape[0]
        wide = jnp.concatenate([sums[0] * row, jnp.zeros((row.shape[0], HD - narrow), jnp.float32)], axis=1)
        kv[...] = wide.T[:narrow].astype(jnp.bfloat16)
        factor[...] = jnp.broadcast_to(row, factor.shape)
    else:
        factor, cosine, sine = extra
        (q,) = refs
        for h in range(q.shape[1] // HD):
            one = sums[0][:, h * HD : (h + 1) * HD] * factor[...]
            turned = one * cosine[...] + pltpu.roll(one, HD // 2, 1) * sine[...]
            q[:, h * HD : (h + 1) * HD] = turned.astype(jnp.bfloat16)


def accumulate(stacks, places, table, gain, wq, wk, wv, prior=(), extra=(), part="all"):
    count = len(places)
    depth = wq.shape[0] // SIDE**2
    rows = sum(s.shape[0] for s in stacks) // count
    parts = [s.shape[0] // rows for s in stacks]
    heads, narrow = wq.shape[1], 2 * wk.shape[0]
    args = list(stacks)
    specs = [whole(s.shape) for s in stacks]
    for k in places:
        args.append(gain)
        specs.append(pl.BlockSpec((1, depth), lambda i, t, k=k: (0, t[k])))
        if part != "kv":
            args.append(wq)
            specs.append(pl.BlockSpec((depth, heads), lambda i, t, k=k: (t[k], 0)))
        if part != "q":
            args += [wk, wv]
            specs += [pl.BlockSpec((narrow // 2, depth), lambda i, t, k=k: (0, t[k]))] * 2
    args += [*prior, *extra]
    specs += [whole(a.shape) for a in (*prior, *extra)]
    sums = [(rows, heads), (rows, narrow), (rows, HD)]
    outs = {
        "all": [(s, jnp.float32) for s in sums],
        "kv": [((narrow, rows), jnp.bfloat16), (sums[2], jnp.float32)],
        "q": [(sums[0], jnp.bfloat16)],
    }[part]
    kernel = functools.partial(
        accumulate_kernel, parts, part, len(prior), len(extra), gain.shape[1]
    )
    return call(kernel, table, args, specs, outs, COST * rows * depth * count * (heads + narrow))


def attend_kernel(place, q, own, right, two, left, cosine, sine, *refs):
    columns, (out, up, down, keys_raw, values) = refs[:SIDE], refs[SIDE:]
    rows = q.shape[0]
    half = rows // 2
    part = own.shape[0] // 2
    for d, piece in enumerate((own, right, two, left)):
        at = pl.multiple_of(lax.rem(place[SIDE**2] + d, SIDE) * part, part)
        keys_raw[pl.ds(at, part), :] = piece[:part]
        values[pl.ds(at, part), :] = piece[part:]
    first = keys_raw[: HD // 2].astype(jnp.float32)
    second = keys_raw[HD // 2 :].astype(jnp.float32)
    keys = jnp.concatenate(
        [
            first * cosine[...] - second * sine[...],
            second * cosine[...] + first * sine[...],
        ],
        axis=0,
    ).astype(jnp.bfloat16)
    seen = lax.broadcasted_iota(jnp.int32, (half, half), 0) >= lax.broadcasted_iota(
        jnp.int32, (half, half), 1
    )
    for i in range(2):
        for h in range(q.shape[1] // HD):
            head = slice(h * HD, (h + 1) * HD)
            mine = q[i * half : (i + 1) * half, head]
            scores = []
            for j in range(i + 1):
                some = dot(mine, keys[:, j * half : (j + 1) * half]) * (1.0 / math.sqrt(HD))
                scores.append(jnp.where(seen, some, jnp.float32(-1e30)) if j == i else some)
            scores = jnp.concatenate(scores, axis=1)
            weights = jnp.exp(scores - jnp.max(scores, axis=1, keepdims=True))
            probs = weights * (1.0 / jnp.sum(weights, axis=1, keepdims=True))
            context = dot(probs.astype(jnp.bfloat16), values[:, : (i + 1) * half], ((1,), (1,)))
            out[i * half : (i + 1) * half, head] = context.astype(jnp.bfloat16)
    for n, weight in enumerate(columns):
        sums = (up, down)[n // 2]
        sums[pl.ds(n % 2 * rows, rows)] = dot(out[...], weight[...]).astype(jnp.bfloat16)


def attend(place, q, parts, cosine, sine, wo, places):
    rows, depth = q.shape
    width = wo.shape[1] // SIDE**2
    args = [q, *parts, cosine, sine]
    specs = [whole(a.shape) for a in args]
    for k in places:
        args.append(wo)
        specs.append(pl.BlockSpec((depth, width), lambda i, t, k=k: (0, t[k])))
    outs = [(q.shape, jnp.bfloat16)] + [((2 * rows, width), jnp.bfloat16)] * 2
    scratch = [pltpu.VMEM((HD, rows), jnp.bfloat16)] * 2
    return call(attend_kernel, place, args, specs, outs, 12 * rows**2 * HD, scratch)


def project_kernel(jobs, base, table, context, *refs):
    refs = list(refs)
    take = lambda n: [refs.pop(0) for _ in range(n)]
    weights = [take(len(job["places"])) for job in jobs]
    arrived = [take(len(job["adds"])) for job in jobs]
    residual = take(1) if base else []
    rows = context.shape[0]
    for job, group, terms in zip(jobs, weights, arrived):
        out = None if job["apart"] else refs.pop(0)
        for n, weight in enumerate(group):
            cut = pl.ds(n * rows, rows)
            value = dot(context[...], weight[...])
            for term in terms:
                value = value + term[cut].astype(jnp.float32)
            if not job["apart"]:
                out[cut] = value.astype(out.dtype)
                continue
            if residual:
                value = value + residual.pop()[...].astype(jnp.float32)
            alone = refs.pop(0)
            alone[...] = value.astype(alone.dtype)


def project(context, wo, table, jobs, base=None):
    rows, depth = context.shape
    width = wo.shape[1] // SIDE**2
    args, specs, outs = [context], [whole(context.shape)], []
    for job in jobs:
        for k in job["places"]:
            args.append(wo)
            specs.append(pl.BlockSpec((depth, width), lambda i, t, k=k: (0, t[k])))
        count = len(job["places"])
        if job["apart"]:
            outs += [((rows, width), jnp.bfloat16)] * count
        else:
            outs.append(((rows * count, width), jnp.bfloat16))
    if base is not None:
        outs[0] = (outs[0][0], jnp.float32)
    more = [a for job in jobs for a in job["adds"]] + ([] if base is None else [base])
    args += more
    specs += [whole(a.shape) for a in more]
    kernel = functools.partial(project_kernel, jobs, base is not None)
    count = sum(len(job["places"]) for job in jobs)
    return call(kernel, table, args, specs, outs, 2 * rows * depth * width * count)


def on_device(tokens, norm_gain, w_query, w_key, w_value, w_output):
    own = tokens[0]
    rows = own.shape[0]
    y, x = lax.axis_index("ty"), lax.axis_index("tx")
    wq, wk, wv, wo = w_query[0], w_key[0].T, w_value[0].T, w_output[0]

    freq = np.exp(np.arange(HD // 2) * (-2.0 * math.log(500000.0) / HD)).astype(np.float32)
    angle = np.arange(rows, dtype=np.float32)[:, None] * freq[None, :]
    cosine = np.concatenate([np.cos(angle)] * 2, axis=1)
    sine = np.concatenate([-np.sin(angle), np.sin(angle)], axis=1)

    far = jnp.array([f + SIDE for f in OFFSETS for _ in OFFSETS], jnp.int32)
    near = jnp.array([n + SIDE for _ in OFFSETS for n in OFFSETS], jnp.int32)
    x_first = lax.rem(lax.axis_index("pp"), 2) == 0
    owners = (y + jnp.where(x_first, far, near)) % SIDE * SIDE
    owners += (x + jnp.where(x_first, near, far)) % SIDE
    owners = jnp.concatenate([owners.astype(jnp.int32), x.astype(jnp.int32)[None]])
    spots = lambda far, *nears: [SIDE * OFFSETS.index(far) + OFFSETS.index(n) for n in nears]
    one, two = (0, -1), (1, 2)

    common = (owners, norm_gain, wq, wk, wv)
    behind, ahead, opposite = (shift(own, SHORT, -d) for d in OFFSETS[1:])
    first = jnp.concatenate([own, behind])
    first_up, first_down = shift(first, LONG, 1), shift(first, LONG, -1)
    second = jnp.concatenate([ahead, opposite])
    second_up, second_down = shift(second, LONG, 1), shift(second, LONG, -1)
    first_far, second_far = shift(first_up, LONG, 1), shift(second_down, LONG, -1)
    sums = accumulate([own, behind, ahead, opposite], spots(0, *one, *two), *common)
    sums = accumulate(
        [first_up, first_down], spots(-1, *one) + spots(1, *one), *common, prior=sums
    )
    sums = accumulate(
        [second_up, second_down], spots(-1, *two) + spots(1, *two), *common, prior=sums
    )
    sums = accumulate([second_far], spots(2, *two), *common, prior=sums)
    stacks, places = [first_far], spots(2, *one)
    kv, row = accumulate(stacks, places, *common, prior=sums[1:], part="kv")
    queries = accumulate(
        stacks, places, *common, prior=sums[:1], extra=(row, cosine, sine), part="q"
    )[0]
    parts = [kv, shift(kv, ROW, -1), shift(kv, ROW, 2), shift(kv, ROW, 1)]
    turns = (np.cos(angle).T.copy(), np.sin(angle).T.copy())
    context, *sent = attend(owners, queries, parts, *turns, wo, spots(2, *one, *two))

    job = lambda far, nears, adds=(), apart=False: dict(
        places=spots(far, *nears), adds=list(adds), apart=apart
    )
    up, down = shift(sent[0], LONG, 1), shift(sent[1], LONG, -1)
    run = functools.partial(project, context, wo, owners)
    sent = run([job(1, two), job(-1, one)])
    two_up, one_down = shift(sent[0], LONG, 1), shift(sent[1], LONG, -1)
    one_up = shift(run([job(1, one, [up])])[0], LONG, 1)
    two_down = shift(run([job(-1, two, [down])])[0], LONG, -1)
    jobs = [job(0, one, [one_up, one_down], True), job(0, two, [two_up, two_down], True)]
    mine, *others = run(jobs, own)
    for d, block in zip(OFFSETS[1:], others):
        mine = mine + shift(block, SHORT, d).astype(jnp.float32)
    step = [(p, (p + 1) % SECTIONS) for p in range(SECTIONS)]
    return lax.ppermute(mine.astype(jnp.bfloat16), "pp", step).astype(jnp.float32)[None]


def solution(mesh):
    shape = mesh.devices.shape
    grid = Mesh(mesh.devices.reshape(SIDE, shape[0] // SIDE, shape[1]), ("ty", "tx", "pp"))
    tp = ("ty", "tx")
    return jax.shard_map(
        on_device,
        mesh=grid,
        in_specs=(
            P("pp", None, tp),
            P("pp", None),
            P("pp", None, tp),
            P("pp", None, tp),
            P("pp", None, tp),
            P("pp", tp, None),
        ),
        out_specs=P("pp", None, tp),
        check_vma=False,
    )
```

```python
import functools
import math

import jax
import jax.numpy as jnp
import numpy as np
from jax import lax
from jax.experimental import pallas as pl
from jax.experimental.pallas import tpu as pltpu
from jax.sharding import Mesh
from jax.sharding import PartitionSpec as P

KVH = 4
HD = 128
SIDE = 4
SECTIONS = 16
EPS = 1e-05
COST = 16
VMEM_BYTES = 20 * 2**20

OFFSETS = (0, -1, 1, 2)


def route(axis_of_core, step):
    pairs = []
    for y in range(SIDE):
        for x in range(SIDE):
            for p in range(SECTIONS):
                along_x = axis_of_core[p % 2] == "tx"
                to_y = y if along_x else (y + step) % SIDE
                to_x = (x + step) % SIDE if along_x else x
                pairs.append(((y * SIDE + x) * SECTIONS + p, (to_y * SIDE + to_x) * SECTIONS + p))
    return pairs


def shift(block, axis_of_core, step):
    return lax.ppermute(block, ("ty", "tx", "pp"), route(axis_of_core, step))


SHORT = ("tx", "ty")
LONG = ("ty", "tx")
ROW = ("tx", "tx")


def dot(a, b, dims=((1,), (0,))):
    return lax.dot_general(a, b, (dims, ((), ())), preferred_element_type=jnp.float32)


def call(kernel, table, args, specs, outs, flops, scratch=()):
    held = sum(math.prod(s.block_shape) for s in specs)
    return pl.pallas_call(
        kernel,
        out_shape=[jax.ShapeDtypeStruct(s, d) for s, d in outs],
        grid_spec=pltpu.PrefetchScalarGridSpec(
            num_scalar_prefetch=1,
            grid=(1,),
            in_specs=specs,
            out_specs=[whole(s) for s, _ in outs],
            scratch_shapes=scratch,
        ),
        compiler_params=pltpu.CompilerParams(vmem_limit_bytes=VMEM_BYTES),
        cost_estimate=pl.CostEstimate(flops=flops, bytes_accessed=4 * held, transcendentals=0),
    )(table, *args)


def whole(shape):
    return pl.BlockSpec(shape, lambda i, t: (0,) * len(shape))


def accumulate_kernel(stacks, part, n_prior, n_extra, width, table, *refs):
    refs = list(refs)
    take = lambda n: [refs.pop(0) for _ in range(n)]
    blocks = []
    for ref, parts in zip(take(len(stacks)), stacks):
        rows = ref.shape[0] // parts
        blocks += [ref.at[pl.ds(n * rows, rows)] for n in range(parts)]
    weights = [take(2 if part == "q" else 4 if part == "all" else 3) for _ in blocks]
    prior, extra = take(n_prior), take(n_extra)
    sums = [ref[...] for ref in prior] or [None] * 3
    for block, (gain, *columns) in zip(blocks, weights):
        x = block[...].astype(jnp.float32)
        scaled = (x * gain[...]).astype(jnp.bfloat16)
        terms = []
        if part != "kv":
            terms.append(dot(scaled, columns[0][...]))
        if part != "q":
            kv_weights = jnp.concatenate([w[...] for w in columns[-2:]], axis=0)
            terms.append(dot(scaled, kv_weights, ((1,), (1,))))
            squares = x * x
            total = squares[:, :128]
            for j in range(1, x.shape[1] // 128):
                total = total + squares[:, j * 128 : (j + 1) * 128]
            terms.append(total)
        sums = [t if s is None else s + t for s, t in zip(sums, terms)]
    if part == "all":
        for ref, value in zip(refs, sums):
            ref[...] = value
    elif part == "kv":
        kv, factor = refs
        row = lax.rsqrt(jnp.sum(sums[1], axis=1, keepdims=True) / width + EPS)
        narrow = kv.shape[0]
        wide = jnp.concatenate([sums[0] * row, jnp.zeros((row.shape[0], HD - narrow), jnp.float32)], axis=1)
        kv[...] = wide.T[:narrow].astype(jnp.bfloat16)
        factor[...] = jnp.broadcast_to(row, factor.shape)
    else:
        factor, cosine, sine = extra
        (q,) = refs
        for h in range(q.shape[1] // HD):
            one = sums[0][:, h * HD : (h + 1) * HD] * factor[...]
            turned = one * cosine[...] + pltpu.roll(one, HD // 2, 1) * sine[...]
            q[:, h * HD : (h + 1) * HD] = turned.astype(jnp.bfloat16)


def accumulate(stacks, places, table, gain, wq, wk, wv, prior=(), extra=(), part="all"):
    count = len(places)
    depth = wq.shape[0] // SIDE**2
    rows = sum(s.shape[0] for s in stacks) // count
    parts = [s.shape[0] // rows for s in stacks]
    heads, narrow = wq.shape[1], 2 * wk.shape[0]
    args = list(stacks)
    specs = [whole(s.shape) for s in stacks]
    for k in places:
        args.append(gain)
        specs.append(pl.BlockSpec((1, depth), lambda i, t, k=k: (0, t[k])))
        if part != "kv":
            args.append(wq)
            specs.append(pl.BlockSpec((depth, heads), lambda i, t, k=k: (t[k], 0)))
        if part != "q":
            args += [wk, wv]
            specs += [pl.BlockSpec((narrow // 2, depth), lambda i, t, k=k: (0, t[k]))] * 2
    args += [*prior, *extra]
    specs += [whole(a.shape) for a in (*prior, *extra)]
    sums = [(rows, heads), (rows, narrow), (rows, HD)]
    outs = {
        "all": [(s, jnp.float32) for s in sums],
        "kv": [((narrow, rows), jnp.bfloat16), (sums[2], jnp.float32)],
        "q": [(sums[0], jnp.bfloat16)],
    }[part]
    kernel = functools.partial(
        accumulate_kernel, parts, part, len(prior), len(extra), gain.shape[1]
    )
    return call(kernel, table, args, specs, outs, COST * rows * depth * count * (heads + narrow))


def attend_kernel(place, q, own, right, two, left, cosine, sine, *refs):
    columns, (out, up, down, keys_raw, values) = refs[:SIDE], refs[SIDE:]
    rows = q.shape[0]
    half = rows // 2
    part = own.shape[0] // 2
    for d, piece in enumerate((own, right, two, left)):
        at = pl.multiple_of(lax.rem(place[SIDE**2] + d, SIDE) * part, part)
        keys_raw[pl.ds(at, part), :] = piece[:part]
        values[pl.ds(at, part), :] = piece[part:]
    first = keys_raw[: HD // 2].astype(jnp.float32)
    second = keys_raw[HD // 2 :].astype(jnp.float32)
    keys = jnp.concatenate(
        [
            first * cosine[...] - second * sine[...],
            second * cosine[...] + first * sine[...],
        ],
        axis=0,
    ).astype(jnp.bfloat16)
    seen = lax.broadcasted_iota(jnp.int32, (half, half), 0) >= lax.broadcasted_iota(
        jnp.int32, (half, half), 1
    )
    for i in range(2):
        for h in range(q.shape[1] // HD):
            head = slice(h * HD, (h + 1) * HD)
            mine = q[i * half : (i + 1) * half, head]
            scores = []
            for j in range(i + 1):
                some = dot(mine, keys[:, j * half : (j + 1) * half]) * (1.0 / math.sqrt(HD))
                scores.append(jnp.where(seen, some, jnp.float32(-1e30)) if j == i else some)
            scores = jnp.concatenate(scores, axis=1)
            weights = jnp.exp(scores - jnp.max(scores, axis=1, keepdims=True))
            probs = weights * (1.0 / jnp.sum(weights, axis=1, keepdims=True))
            context = dot(probs.astype(jnp.bfloat16), values[:, : (i + 1) * half], ((1,), (1,)))
            out[i * half : (i + 1) * half, head] = context.astype(jnp.bfloat16)
    for n, weight in enumerate(columns):
        sums = (up, down)[n // 2]
        sums[pl.ds(n % 2 * rows, rows)] = dot(out[...], weight[...]).astype(jnp.bfloat16)


def attend(place, q, parts, cosine, sine, wo, places):
    rows, depth = q.shape
    width = wo.shape[1] // SIDE**2
    args = [q, *parts, cosine, sine]
    specs = [whole(a.shape) for a in args]
    for k in places:
        args.append(wo)
        specs.append(pl.BlockSpec((depth, width), lambda i, t, k=k: (0, t[k])))
    outs = [(q.shape, jnp.bfloat16)] + [((2 * rows, width), jnp.bfloat16)] * 2
    scratch = [pltpu.VMEM((HD, rows), jnp.bfloat16)] * 2
    return call(attend_kernel, place, args, specs, outs, 12 * rows**2 * HD, scratch)


def project_kernel(jobs, base, table, context, *refs):
    refs = list(refs)
    take = lambda n: [refs.pop(0) for _ in range(n)]
    weights = [take(len(job["places"])) for job in jobs]
    arrived = [take(len(job["adds"])) for job in jobs]
    residual = take(1) if base else []
    rows = context.shape[0]
    for job, group, terms in zip(jobs, weights, arrived):
        out = None if job["apart"] else refs.pop(0)
        for n, weight in enumerate(group):
            cut = pl.ds(n * rows, rows)
            value = dot(context[...], weight[...])
            for term in terms:
                value = value + term[cut].astype(jnp.float32)
            if not job["apart"]:
                out[cut] = value.astype(out.dtype)
                continue
            if residual:
                value = value + residual.pop()[...].astype(jnp.float32)
            for h in range(2):
                alone = refs.pop(0)
                alone[...] = value[h * rows // 2 : (h + 1) * rows // 2].astype(alone.dtype)


def project(context, wo, table, jobs, base=None):
    rows, depth = context.shape
    width = wo.shape[1] // SIDE**2
    args, specs, outs = [context], [whole(context.shape)], []
    for job in jobs:
        for k in job["places"]:
            args.append(wo)
            specs.append(pl.BlockSpec((depth, width), lambda i, t, k=k: (0, t[k])))
        count = len(job["places"])
        if job["apart"]:
            outs += [((rows // 2, width), jnp.bfloat16)] * (2 * count)
        else:
            outs.append(((rows * count, width), jnp.bfloat16))
    if base is not None:
        outs[:2] = [(outs[0][0], jnp.float32)] * 2
    more = [a for job in jobs for a in job["adds"]] + ([] if base is None else [base])
    args += more
    specs += [whole(a.shape) for a in more]
    kernel = functools.partial(project_kernel, jobs, base is not None)
    count = sum(len(job["places"]) for job in jobs)
    return call(kernel, table, args, specs, outs, 2 * rows * depth * width * count)


def on_device(tokens, norm_gain, w_query, w_key, w_value, w_output):
    own = tokens[0]
    rows = own.shape[0]
    y, x = lax.axis_index("ty"), lax.axis_index("tx")
    wq, wk, wv, wo = w_query[0], w_key[0].T, w_value[0].T, w_output[0]

    freq = np.exp(np.arange(HD // 2) * (-2.0 * math.log(500000.0) / HD)).astype(np.float32)
    angle = np.arange(rows, dtype=np.float32)[:, None] * freq[None, :]
    cosine = np.concatenate([np.cos(angle)] * 2, axis=1)
    sine = np.concatenate([-np.sin(angle), np.sin(angle)], axis=1)

    far = jnp.array([f + SIDE for f in OFFSETS for _ in OFFSETS], jnp.int32)
    near = jnp.array([n + SIDE for _ in OFFSETS for n in OFFSETS], jnp.int32)
    x_first = lax.rem(lax.axis_index("pp"), 2) == 0
    owners = (y + jnp.where(x_first, far, near)) % SIDE * SIDE
    owners += (x + jnp.where(x_first, near, far)) % SIDE
    owners = jnp.concatenate([owners.astype(jnp.int32), x.astype(jnp.int32)[None]])
    spots = lambda far, *nears: [SIDE * OFFSETS.index(far) + OFFSETS.index(n) for n in nears]
    one, two = (0, -1), (1, 2)

    common = (owners, norm_gain, wq, wk, wv)
    behind, ahead, opposite = (shift(own, SHORT, -d) for d in OFFSETS[1:])
    first = jnp.concatenate([own, behind])
    first_up, first_down = shift(first, LONG, 1), shift(first, LONG, -1)
    second = jnp.concatenate([ahead, opposite])
    second_up, second_down = shift(second, LONG, 1), shift(second, LONG, -1)
    first_far, second_far = shift(first_up, LONG, 1), shift(second_down, LONG, -1)
    sums = accumulate([own, behind, ahead, opposite], spots(0, *one, *two), *common)
    sums = accumulate(
        [first_up, first_down], spots(-1, *one) + spots(1, *one), *common, prior=sums
    )
    sums = accumulate(
        [second_up, second_down], spots(-1, *two) + spots(1, *two), *common, prior=sums
    )
    sums = accumulate([second_far], spots(2, *two), *common, prior=sums)
    stacks, places = [first_far], spots(2, *one)
    kv, row = accumulate(stacks, places, *common, prior=sums[1:], part="kv")
    queries = accumulate(
        stacks, places, *common, prior=sums[:1], extra=(row, cosine, sine), part="q"
    )[0]
    parts = [kv, shift(kv, ROW, -1), shift(kv, ROW, 2), shift(kv, ROW, 1)]
    turns = (np.cos(angle).T.copy(), np.sin(angle).T.copy())
    context, *sent = attend(owners, queries, parts, *turns, wo, spots(2, *one, *two))

    job = lambda far, nears, adds=(), apart=False: dict(
        places=spots(far, *nears), adds=list(adds), apart=apart
    )
    up, down = shift(sent[0], LONG, 1), shift(sent[1], LONG, -1)
    run = functools.partial(project, context, wo, owners)
    sent = run([job(1, two), job(-1, one)])
    two_up, one_down = shift(sent[0], LONG, 1), shift(sent[1], LONG, -1)
    one_up = shift(run([job(1, one, [up])])[0], LONG, 1)
    two_down = shift(run([job(-1, two, [down])])[0], LONG, -1)
    jobs = [job(0, one, [one_up, one_down], True), job(0, two, [two_up, two_down], True)]
    pieces = run(jobs, own)
    step = [(p, (p + 1) % SECTIONS) for p in range(SECTIONS)]
    results = []
    for h in range(2):
        mine, *others = pieces[h::2]
        for d, block in zip(OFFSETS[1:], others):
            mine = mine + shift(block, SHORT, d).astype(jnp.float32)
        results.append(lax.ppermute(mine.astype(jnp.bfloat16), "pp", step).astype(jnp.float32))
    return jnp.concatenate(results)[None]


def solution(mesh):
    shape = mesh.devices.shape
    grid = Mesh(mesh.devices.reshape(SIDE, shape[0] // SIDE, shape[1]), ("ty", "tx", "pp"))
    tp = ("ty", "tx")
    return jax.shard_map(
        on_device,
        mesh=grid,
        in_specs=(
            P("pp", None, tp),
            P("pp", None),
            P("pp", None, tp),
            P("pp", None, tp),
            P("pp", None, tp),
            P("pp", tp, None),
        ),
        out_specs=P("pp", None, tp),
        check_vma=False,
    )
```

```python
import functools
import math

import jax
import jax.numpy as jnp
import numpy as np
from jax import lax
from jax.experimental import pallas as pl
from jax.experimental.pallas import tpu as pltpu
from jax.sharding import Mesh
from jax.sharding import PartitionSpec as P

KVH = 4
HD = 128
SIDE = 4
SECTIONS = 16
EPS = 1e-05
COST = 16
VMEM_BYTES = 20 * 2**20

OFFSETS = (0, -1, 1, 2)


def route(axis_of_core, step):
    pairs = []
    for y in range(SIDE):
        for x in range(SIDE):
            for p in range(SECTIONS):
                along_x = axis_of_core[p % 2] == "tx"
                to_y = y if along_x else (y + step) % SIDE
                to_x = (x + step) % SIDE if along_x else x
                pairs.append(((y * SIDE + x) * SECTIONS + p, (to_y * SIDE + to_x) * SECTIONS + p))
    return pairs


def shift(block, axis_of_core, step):
    return lax.ppermute(block, ("ty", "tx", "pp"), route(axis_of_core, step))


SHORT = ("tx", "ty")
LONG = ("ty", "tx")
ROW = ("tx", "tx")


def dot(a, b, dims=((1,), (0,))):
    return lax.dot_general(a, b, (dims, ((), ())), preferred_element_type=jnp.float32)


def call(kernel, table, args, specs, outs, flops, scratch=()):
    held = sum(math.prod(s.block_shape) for s in specs)
    return pl.pallas_call(
        kernel,
        out_shape=[jax.ShapeDtypeStruct(s, d) for s, d in outs],
        grid_spec=pltpu.PrefetchScalarGridSpec(
            num_scalar_prefetch=1,
            grid=(1,),
            in_specs=specs,
            out_specs=[whole(s) for s, _ in outs],
            scratch_shapes=scratch,
        ),
        compiler_params=pltpu.CompilerParams(vmem_limit_bytes=VMEM_BYTES),
        cost_estimate=pl.CostEstimate(flops=flops, bytes_accessed=4 * held, transcendentals=0),
    )(table, *args)


def whole(shape):
    return pl.BlockSpec(shape, lambda i, t: (0,) * len(shape))


def accumulate_kernel(stacks, part, n_prior, n_extra, width, table, *refs):
    refs = list(refs)
    take = lambda n: [refs.pop(0) for _ in range(n)]
    blocks = []
    for ref, parts in zip(take(len(stacks)), stacks):
        rows = ref.shape[0] // parts
        blocks += [ref.at[pl.ds(n * rows, rows)] for n in range(parts)]
    weights = [take(2 if part == "q" else 4 if part == "all" else 3) for _ in blocks]
    prior, extra = take(n_prior), take(n_extra)
    sums = [ref[...] for ref in prior] or [None] * 3
    for block, (gain, *columns) in zip(blocks, weights):
        x = block[...].astype(jnp.float32)
        scaled = (x * gain[...]).astype(jnp.bfloat16)
        terms = []
        if part != "kv":
            terms.append(dot(scaled, columns[0][...]))
        if part != "q":
            kv_weights = jnp.concatenate([w[...] for w in columns[-2:]], axis=0)
            terms.append(dot(scaled, kv_weights, ((1,), (1,))))
            squares = x * x
            total = squares[:, :128]
            for j in range(1, x.shape[1] // 128):
                total = total + squares[:, j * 128 : (j + 1) * 128]
            terms.append(total)
        sums = [t if s is None else s + t for s, t in zip(sums, terms)]
    if part == "all":
        for ref, value in zip(refs, sums):
            ref[...] = value
    elif part == "kv":
        kv, factor = refs
        row = lax.rsqrt(jnp.sum(sums[1], axis=1, keepdims=True) / width + EPS)
        narrow = kv.shape[0]
        wide = jnp.concatenate([sums[0] * row, jnp.zeros((row.shape[0], HD - narrow), jnp.float32)], axis=1)
        kv[...] = wide.T[:narrow].astype(jnp.bfloat16)
        factor[...] = jnp.broadcast_to(row, factor.shape)
    else:
        factor, cosine, sine = extra
        (q,) = refs
        for h in range(q.shape[1] // HD):
            one = sums[0][:, h * HD : (h + 1) * HD] * factor[...]
            turned = one * cosine[...] + pltpu.roll(one, HD // 2, 1) * sine[...]
            q[:, h * HD : (h + 1) * HD] = turned.astype(jnp.bfloat16)


def accumulate(stacks, places, table, gain, wq, wk, wv, prior=(), extra=(), part="all"):
    count = len(places)
    depth = wq.shape[0] // SIDE**2
    rows = sum(s.shape[0] for s in stacks) // count
    parts = [s.shape[0] // rows for s in stacks]
    heads, narrow = wq.shape[1], 2 * wk.shape[0]
    args = list(stacks)
    specs = [whole(s.shape) for s in stacks]
    for k in places:
        args.append(gain)
        specs.append(pl.BlockSpec((1, depth), lambda i, t, k=k: (0, t[k])))
        if part != "kv":
            args.append(wq)
            specs.append(pl.BlockSpec((depth, heads), lambda i, t, k=k: (t[k], 0)))
        if part != "q":
            args += [wk, wv]
            specs += [pl.BlockSpec((narrow // 2, depth), lambda i, t, k=k: (0, t[k]))] * 2
    args += [*prior, *extra]
    specs += [whole(a.shape) for a in (*prior, *extra)]
    sums = [(rows, heads), (rows, narrow), (rows, HD)]
    outs = {
        "all": [(s, jnp.float32) for s in sums],
        "kv": [((narrow, rows), jnp.bfloat16), (sums[2], jnp.float32)],
        "q": [(sums[0], jnp.bfloat16)],
    }[part]
    kernel = functools.partial(
        accumulate_kernel, parts, part, len(prior), len(extra), gain.shape[1]
    )
    return call(kernel, table, args, specs, outs, COST * rows * depth * count * (heads + narrow))


def attend_kernel(place, q, own, right, two, left, cosine, sine, *refs):
    columns, (out, up, down, keys_raw, values) = refs[:SIDE], refs[SIDE:]
    rows = q.shape[0]
    half = rows // 2
    part = own.shape[0] // 2
    for d, piece in enumerate((own, right, two, left)):
        at = pl.multiple_of(lax.rem(place[SIDE**2] + d, SIDE) * part, part)
        keys_raw[pl.ds(at, part), :] = piece[:part]
        values[pl.ds(at, part), :] = piece[part:]
    first = keys_raw[: HD // 2].astype(jnp.float32)
    second = keys_raw[HD // 2 :].astype(jnp.float32)
    keys = jnp.concatenate(
        [
            first * cosine[...] - second * sine[...],
            second * cosine[...] + first * sine[...],
        ],
        axis=0,
    ).astype(jnp.bfloat16)
    seen = lax.broadcasted_iota(jnp.int32, (half, half), 0) >= lax.broadcasted_iota(
        jnp.int32, (half, half), 1
    )
    for i in range(2):
        for h in range(q.shape[1] // HD):
            head = slice(h * HD, (h + 1) * HD)
            mine = q[i * half : (i + 1) * half, head]
            scores = []
            for j in range(i + 1):
                some = dot(mine, keys[:, j * half : (j + 1) * half]) * (1.0 / math.sqrt(HD))
                scores.append(jnp.where(seen, some, jnp.float32(-1e30)) if j == i else some)
            scores = jnp.concatenate(scores, axis=1)
            weights = jnp.exp(scores - jnp.max(scores, axis=1, keepdims=True))
            probs = weights * (1.0 / jnp.sum(weights, axis=1, keepdims=True))
            context = dot(probs.astype(jnp.bfloat16), values[:, : (i + 1) * half], ((1,), (1,)))
            out[i * half : (i + 1) * half, head] = context.astype(jnp.bfloat16)
    for n, weight in enumerate(columns):
        sums = (up, down)[n // 2]
        sums[pl.ds(n % 2 * rows, rows)] = dot(out[...], weight[...]).astype(jnp.bfloat16)


def attend(place, q, parts, cosine, sine, wo, places):
    rows, depth = q.shape
    width = wo.shape[1] // SIDE**2
    args = [q, *parts, cosine, sine]
    specs = [whole(a.shape) for a in args]
    for k in places:
        args.append(wo)
        specs.append(pl.BlockSpec((depth, width), lambda i, t, k=k: (0, t[k])))
    outs = [(q.shape, jnp.bfloat16)] + [((2 * rows, width), jnp.bfloat16)] * 2
    scratch = [pltpu.VMEM((HD, rows), jnp.bfloat16)] * 2
    return call(attend_kernel, place, args, specs, outs, 12 * rows**2 * HD, scratch)


def project_kernel(jobs, base, table, context, *refs):
    refs = list(refs)
    take = lambda n: [refs.pop(0) for _ in range(n)]
    weights = [take(len(job["places"])) for job in jobs]
    arrived = [take(len(job["adds"])) for job in jobs]
    residual = take(1) if base else []
    rows = context.shape[0]
    for job, group, terms in zip(jobs, weights, arrived):
        out = None if job["apart"] else refs.pop(0)
        for n, weight in enumerate(group):
            cut = pl.ds(n * rows, rows)
            value = dot(context[...], weight[...])
            for term in terms:
                value = value + term[cut].astype(jnp.float32)
            if not job["apart"]:
                out[cut] = value.astype(out.dtype)
                continue
            if residual:
                value = value + residual.pop()[...].astype(jnp.float32)
            begin = 0
            for _ in range(2):
                alone = refs.pop(0)
                end = begin + alone.shape[0]
                alone[...] = value[begin:end].astype(alone.dtype)
                begin = end


def project(context, wo, table, jobs, base=None):
    rows, depth = context.shape
    width = wo.shape[1] // SIDE**2
    args, specs, outs = [context], [whole(context.shape)], []
    for job in jobs:
        for k in job["places"]:
            args.append(wo)
            specs.append(pl.BlockSpec((depth, width), lambda i, t, k=k: (0, t[k])))
        count = len(job["places"])
        if job["apart"]:
            cuts = (rows * 5 // 8, rows * 3 // 8)
            outs += [((cut, width), jnp.bfloat16) for cut in cuts] * count
        else:
            outs.append(((rows * count, width), jnp.bfloat16))
    if base is not None:
        outs[:2] = [(shape, jnp.float32) for shape, _ in outs[:2]]
    more = [a for job in jobs for a in job["adds"]] + ([] if base is None else [base])
    args += more
    specs += [whole(a.shape) for a in more]
    kernel = functools.partial(project_kernel, jobs, base is not None)
    count = sum(len(job["places"]) for job in jobs)
    return call(kernel, table, args, specs, outs, 2 * rows * depth * width * count)


def on_device(tokens, norm_gain, w_query, w_key, w_value, w_output):
    own = tokens[0]
    rows = own.shape[0]
    y, x = lax.axis_index("ty"), lax.axis_index("tx")
    wq, wk, wv, wo = w_query[0], w_key[0].T, w_value[0].T, w_output[0]

    freq = np.exp(np.arange(HD // 2) * (-2.0 * math.log(500000.0) / HD)).astype(np.float32)
    angle = np.arange(rows, dtype=np.float32)[:, None] * freq[None, :]
    cosine = np.concatenate([np.cos(angle)] * 2, axis=1)
    sine = np.concatenate([-np.sin(angle), np.sin(angle)], axis=1)

    far = jnp.array([f + SIDE for f in OFFSETS for _ in OFFSETS], jnp.int32)
    near = jnp.array([n + SIDE for _ in OFFSETS for n in OFFSETS], jnp.int32)
    x_first = lax.rem(lax.axis_index("pp"), 2) == 0
    owners = (y + jnp.where(x_first, far, near)) % SIDE * SIDE
    owners += (x + jnp.where(x_first, near, far)) % SIDE
    owners = jnp.concatenate([owners.astype(jnp.int32), x.astype(jnp.int32)[None]])
    spots = lambda far, *nears: [SIDE * OFFSETS.index(far) + OFFSETS.index(n) for n in nears]
    one, two = (0, -1), (1, 2)

    common = (owners, norm_gain, wq, wk, wv)
    behind, ahead, opposite = (shift(own, SHORT, -d) for d in OFFSETS[1:])
    first = jnp.concatenate([own, behind])
    first_up, first_down = shift(first, LONG, 1), shift(first, LONG, -1)
    second = jnp.concatenate([ahead, opposite])
    second_up, second_down = shift(second, LONG, 1), shift(second, LONG, -1)
    first_far, second_far = shift(first_up, LONG, 1), shift(second_down, LONG, -1)
    sums = accumulate([own, behind, ahead, opposite], spots(0, *one, *two), *common)
    sums = accumulate(
        [first_up, first_down], spots(-1, *one) + spots(1, *one), *common, prior=sums
    )
    sums = accumulate(
        [second_up, second_down], spots(-1, *two) + spots(1, *two), *common, prior=sums
    )
    sums = accumulate([second_far], spots(2, *two), *common, prior=sums)
    stacks, places = [first_far], spots(2, *one)
    kv, row = accumulate(stacks, places, *common, prior=sums[1:], part="kv")
    queries = accumulate(
        stacks, places, *common, prior=sums[:1], extra=(row, cosine, sine), part="q"
    )[0]
    parts = [kv, shift(kv, ROW, -1), shift(kv, ROW, 2), shift(kv, ROW, 1)]
    turns = (np.cos(angle).T.copy(), np.sin(angle).T.copy())
    context, *sent = attend(owners, queries, parts, *turns, wo, spots(2, *one, *two))

    job = lambda far, nears, adds=(), apart=False: dict(
        places=spots(far, *nears), adds=list(adds), apart=apart
    )
    up, down = shift(sent[0], LONG, 1), shift(sent[1], LONG, -1)
    run = functools.partial(project, context, wo, owners)
    sent = run([job(1, two), job(-1, one)])
    two_up, one_down = shift(sent[0], LONG, 1), shift(sent[1], LONG, -1)
    one_up = shift(run([job(1, one, [up])])[0], LONG, 1)
    two_down = shift(run([job(-1, two, [down])])[0], LONG, -1)
    jobs = [job(0, one, [one_up, one_down], True), job(0, two, [two_up, two_down], True)]
    pieces = run(jobs, own)
    step = [(p, (p + 1) % SECTIONS) for p in range(SECTIONS)]
    results = []
    for h in range(2):
        mine, *others = pieces[h::2]
        for d, block in zip(OFFSETS[1:], others):
            mine = mine + shift(block, SHORT, d).astype(jnp.float32)
        results.append(lax.ppermute(mine.astype(jnp.bfloat16), "pp", step).astype(jnp.float32))
    return jnp.concatenate(results)[None]


def solution(mesh):
    shape = mesh.devices.shape
    grid = Mesh(mesh.devices.reshape(SIDE, shape[0] // SIDE, shape[1]), ("ty", "tx", "pp"))
    tp = ("ty", "tx")
    return jax.shard_map(
        on_device,
        mesh=grid,
        in_specs=(
            P("pp", None, tp),
            P("pp", None),
            P("pp", None, tp),
            P("pp", None, tp),
            P("pp", None, tp),
            P("pp", tp, None),
        ),
        out_specs=P("pp", None, tp),
        check_vma=False,
    )
```
